256 devices in a mesh: dp: 8 (over y, core), vocab: 32 (over x, z).
Axes of the slice: x: 4, y: 4, z: 8, core: 2. Of those that a mesh axis runs over, the one named last changes fastest.
Arguments:
- grads: bfloat16 [8, 8192, 4608], P('dp', 'vocab'), may hold values from -6 to 6
- errors: bfloat16 [8, 8192, 4608], P('dp', 'vocab'), may hold values from -4 to 4
- start_q: float32 [4608, 32], replicated, may hold values from -6 to 6
Outputs:
- right_factor: float32 [4608, 32], replicated
- new_errors: bfloat16 [8, 8192, 4608], P('dp', 'vocab')
The draws below stay inside these ranges and needn't reach their ends.
All inputs are finite; a program needn't handle non-finite values.
Results may differ from the reference program's by a relative error of at most 0.001.
Values sent between devices are 32-bit elements; how exact they have to be, the bound alone decides.
A program may use at most 64 MiB of HBM per device.

```python
import jax
import jax.numpy as jnp
from jax import lax

D = 4608
RANK = 32
ITERS = 2
ROWS = 8192
REPLICAS = 8


def level_of(own_key, extent, shards, smallest, high):
    factor_of, own = 1.0, jax.random.fold_in(own_key, 6)
    for position, parts in shards:
        draws = jnp.exp(jax.random.uniform(jax.random.fold_in(own, position), (parts,), jnp.float32, smallest / len(shards), high / len(shards)))
        factor_of = factor_of * jnp.repeat(draws, extent[position] // parts).reshape([-1 if axis == position else 1 for axis in range(len(extent))])
    return factor_of


def bell_draw(own_key, extent, deviation, limit, split=(), kind=jnp.bfloat16):
    drawn = jax.random.normal(own_key, extent, jnp.float32) * deviation
    if len(split) > 0:
        drawn = level_of(own_key, extent, split, -0.22, 0.18) * drawn
    return jnp.clip(drawn, min=-limit, max=limit).astype(kind)


def setup_inputs(seed: int = 0) -> dict:
    key_list = jax.random.split(jax.random.key(seed), 4)
    return {
        "grads": bell_draw(key_list[0], (REPLICAS, ROWS, D), 1.0, 6.0, ((0, 8), (1, 32))),
        "errors": bell_draw(key_list[1], (REPLICAS, ROWS, D), 0.5, 4.0, ((0, 8), (1, 32))),
        "start_q": bell_draw(key_list[2], (D, RANK), 1.0, 6.0, (), jnp.float32),
    }


def reference(grads, errors, start_q):
    hi = lax.Precision.HIGHEST

    def mixed_at(index):
        return grads[index].astype(jnp.float32) + errors[index].astype(jnp.float32)
    q_now = start_q
    basis = None
    for step in range(ITERS):

        def add_left(index, total):
            return total + jnp.dot(mixed_at(index), q_now, precision=hi)
        left = lax.fori_loop(0, REPLICAS, add_left, jnp.zeros((ROWS, RANK), jnp.float32))
        gram = jnp.dot(left.T, left, precision=hi)
        lower = jnp.linalg.cholesky(gram)
        basis = lax.linalg.triangular_solve(lower, left, left_side=False, lower=True, transpose_a=True)

        def add_right(index, total):
            return total + jnp.dot(mixed_at(index).T, basis, precision=hi)
        q_now = lax.fori_loop(0, REPLICAS, add_right, jnp.zeros((D, RANK), jnp.float32)) / REPLICAS
    approx = jnp.dot(basis, q_now.T, precision=hi)

    def fresh(index):
        return (mixed_at(index) - approx).astype(jnp.bfloat16)
    new_errors = lax.map(fresh, jnp.arange(REPLICAS, dtype=jnp.int32))
    return (q_now, new_errors)
```

```python
import functools

import jax
import jax.numpy as jnp
from jax import lax
from jax.experimental import pallas as pl
from jax.experimental.pallas import tpu as pltpu
from jax.sharding import PartitionSpec as P

MESH = pl.DeviceIdType.MESH
F32, BF16 = jnp.float32, jnp.bfloat16
ITERS = 2
RANK = 32
LANES = 128
STEP = 768
WINDOW = 5
Y, X, Z = 4, 4, 8
PLANE = Y * X


def split(value):
    high = value.astype(BF16)
    rest = value - high.astype(F32)
    middle = rest.astype(BF16)
    return high, middle, (rest - middle.astype(F32)).astype(BF16)


def dot(a, b, over_a, over_b):
    return lax.dot_general(a, b, (((over_a,), (over_b,)), ((), ())), preferred_element_type=F32)


def lower_inverse(packed):
    row = lax.broadcasted_iota(jnp.int32, (RANK, LANES), 0)
    lane = lax.broadcasted_iota(jnp.int32, (RANK, LANES), 1)
    turned = [packed if r == 1 else pltpu.roll(packed, (RANK - RANK * r) % LANES, 1) for r in range(4)]
    work = jnp.where(lane < RANK, jnp.where(lane == row, 1.0, 0.0), jnp.concatenate(turned, axis=0))
    rows = row[:, :1]
    pivots = jnp.ones((RANK, 1), F32)
    for j in range(RANK):
        column, pivot = work[:, RANK + j : RANK + j + 1], work[j : j + 1, RANK + j : RANK + j + 1]
        factor = jnp.where(rows > j, column / pivot, 0.0)
        pivots = jnp.where(rows == j, pivot, pivots)
        work = work - factor * work[j : j + 1, :]
    return (work * lax.rsqrt(pivots))[:, :RANK]


def six(value):
    high, middle, low = split(value)
    return jnp.concatenate([high, high, high, middle, middle, low], axis=1)


def six_rows(value):
    high, middle, low = split(value)
    return jnp.concatenate([high, middle, low, high, middle, high], axis=0)


def kernel(
    g_hbm, e_hbm, q_ref, rf_hbm, o_hbm,
    g, e, o, rf, lp, lr, ly, gx, u, pr, s, rs, zb, ag,
    load_sem, out_sem, send_sem, recv_sem,
):
    dp, vocab = lax.axis_index("dp"), lax.axis_index("vocab")
    y, c, x, z = dp // 2, lax.rem(dp, 2), vocab // Z, lax.rem(vocab, Z)
    mine = y * X + x
    columns = g.shape[1]
    half = columns // 2
    tiles = half // LANES

    def device(y, c, x, z):
        return (y * 2 + c, x * Z + z)

    sibling = device(y, 1 - c, x, z)
    y_peers = [device(lax.rem(y + k, Y), c, x, z) for k in range(1, Y)]
    x_peers = [device(y, c, lax.rem(x + k, X), z) for k in range(1, X)]
    z_peers = [device(y, c, x, lax.rem(z + k, Z)) for k in range(1, Z)]
    places = [lax.rem(mine + k, PLANE) for k in range(1, PLANE)]
    plane_peers = [device(p // X, c, lax.rem(p, X), z) for p in places]

    loads = []
    for k in range(columns // STEP):
        part = pl.ds(k * STEP, STEP)
        loads.append([
            pltpu.make_async_copy(hbm.at[:, part], vmem.at[:, part], load_sem.at[n, k])
            for n, (hbm, vmem) in enumerate(((g_hbm, g), (e_hbm, e)))
        ])
        for copy in loads[-1]:
            copy.start()

    barrier = pltpu.get_barrier_semaphore()
    everyone = [sibling] + plane_peers + z_peers
    for peer in everyone:
        pl.semaphore_signal(barrier, inc=1, device_id=peer, device_id_type=MESH)

    sent = []

    def send(src, dst, peers, phase):
        sources = src if isinstance(src, list) else [src] * len(peers)
        for source, peer in zip(sources, peers):
            pltpu.make_async_remote_copy(
                src_ref=source, dst_ref=dst, send_sem=send_sem.at[phase], recv_sem=recv_sem.at[phase],
                device_id=peer, device_id_type=MESH,
            ).start()

    def arrive(whole, phase):
        pltpu.make_async_copy(whole, whole, recv_sem.at[phase]).wait()
        sent.append((whole, phase))

    def columns_of(which, k):
        return pl.ds(pl.multiple_of(which * half + k * STEP, LANES), STEP)

    def gathered(it, which, k):
        parts = []
        for column in range(k * STEP // LANES, (k + 1) * STEP // LANES):
            rows = []
            for r in range(4):
                tile = column * 4 + r
                pair, at = tile // 9, tile % 9
                place, at = (2 * pair, at) if at < WINDOW else (2 * pair + 1, at - WINDOW + 1)
                rows.append(ag[it, which, place, at])
            parts.append(jnp.concatenate(rows, axis=0))
        return jnp.concatenate(parts, axis=1)

    def left_part(total, q, where):
        q3 = jnp.concatenate(split(q), axis=0)
        return total + (dot(g[:, where], q3, 1, 1) + dot(e[:, where], q3, 1, 1))

    def right_half(it, l3, which):
        for k in range(half // STEP):
            where = columns_of(which, k)
            part = dot(l3, g[:, where], 1, 0) + dot(l3, e[:, where], 1, 0)
            part = part[:RANK] + part[RANK : 2 * RANK] + part[2 * RANK :]
            for n in range(STEP // LANES):
                tile = (k * STEP // LANES + n) * 4
                u[it, which, tile : tile + 4] = part[:, n * LANES : (n + 1) * LANES].reshape(4, 8, LANES)

    total = jnp.zeros((g.shape[0], 3 * RANK), F32)
    inverse = None
    for it in range(ITERS):
        base = 8 * it
        if it == 0:
            for k in range(columns // STEP):
                for copy in loads[k]:
                    copy.wait()
                where = pl.ds(k * STEP, STEP)
                total = left_part(total, q_ref[:, where], where)
            pl.semaphore_wait(barrier, len(everyone))
        else:
            total = jnp.zeros_like(total)
            for k in range(half // STEP):
                total = left_part(total, gathered(it - 1, c, k), columns_of(c, k))
            arrive(ag.at[it - 1, 1 - c], base - 1)
            for k in range(half // STEP):
                total = left_part(total, gathered(it - 1, 1 - c, k), columns_of(1 - c, k))
        turned = jnp.concatenate([total, jnp.zeros((g.shape[0], LANES - 3 * RANK), F32)], axis=1).T
        lp[it] = turned[:RANK] + turned[RANK : 2 * RANK] + turned[2 * RANK : 3 * RANK]
        send(lp.at[it], lr.at[it], [sibling], base)
        arrive(lr.at[it], base)
        ly[it, y] = lp[it] + lr[it]
        send(ly.at[it, y], ly.at[it, y], y_peers, base + 1)
        arrive(ly.at[it, pl.ds(0, Y - 1)], base + 1)
        left = ly[it, 0] + ly[it, 1] + ly[it, 2] + ly[it, 3]
        if it > 0:
            left = dot(six(inverse * 0.125), six_rows(left), 1, 0)

        high, middle, low = split(left)
        other = jnp.concatenate([high, middle, low, high, middle, high], axis=1)
        square = dot(
            jnp.concatenate([high, high, high, middle, middle, low], axis=1),
            jnp.concatenate([other] * 4, axis=0), 1, 1,
        )
        lane = lax.broadcasted_iota(jnp.int32, (8, LANES), 1) // RANK
        packed = square[0:8]
        for r in range(1, 4):
            packed = jnp.where(lane == r, square[8 * r : 8 * r + 8], packed)
        gx[it, x] = packed
        send(gx.at[it, x], gx.at[it, x], x_peers, base + 2)

        l3 = jnp.concatenate([high, middle, low], axis=0)
        right_half(it, l3, 1 - c)
        send(u.at[it, 1 - c], pr.at[it], [sibling], base + 3)
        right_half(it, l3, c)
        arrive(pr.at[it], base + 3)
        s[it] = u[it, c] + pr[it]
        send([s.at[it, pl.ds(9 * p // 2, WINDOW)] for p in places], rs.at[it, mine], plane_peers, base + 4)
        rs[it, mine] = s[it, pl.ds(9 * mine // 2, WINDOW)]
        arrive(gx.at[it, pl.ds(0, X - 1)], base + 2)
        zb[it, z, WINDOW] = gx[it, 0] + gx[it, 1] + gx[it, 2] + gx[it, 3]
        arrive(rs.at[it, pl.ds(0, PLANE - 1)], base + 4)
        piece = rs[it, 0]
        for p in range(1, PLANE):
            piece = piece + rs[it, p]
        zb[it, z, 0:WINDOW] = piece
        send(zb.at[it, z], zb.at[it, z], z_peers, base + 5)
        arrive(zb.at[it, pl.ds(0, Z - 1)], base + 5)
        piece = zb[it, 0]
        for p in range(1, Z):
            piece = piece + zb[it, p]
        ag[it, c, mine] = piece[:WINDOW]
        send(ag.at[it, c, mine], ag.at[it, c, mine], plane_peers, base + 6)
        inverse = lower_inverse(piece[WINDOW])
        arrive(ag.at[it, c, pl.ds(0, PLANE - 1)], base + 6)
        send(ag.at[it, c], ag.at[it, c], [sibling], base + 7)

    last = ITERS - 1
    inverse6 = six(inverse)
    high, middle, _ = split(dot(inverse6, six_rows(left), 1, 0))
    basis3 = jnp.concatenate([high, high, middle], axis=0).astype(F32).T.astype(BF16)
    inverse6 = (inverse6.astype(F32) * 0.125).astype(BF16)
    outs = []
    for which in (c, 1 - c):
        if len(outs) > 0:
            arrive(ag.at[last, 1 - c], 8 * last + 7)
        for k in range(half // STEP):
            where = columns_of(which, k)
            right = dot(inverse6, six_rows(gathered(last, which, k)), 1, 0)
            rf[:, where] = right
            high, middle, _ = split(right)
            approx = dot(basis3, jnp.concatenate([high, middle, high], axis=0), 1, 0)
            o[:, where] = (g[:, where].astype(F32) + e[:, where].astype(F32) - approx).astype(BF16)
            n = len(outs)
            outs.append((
                pltpu.make_async_copy(o.at[:, where], o_hbm.at[:, where], out_sem.at[0, n]),
                pltpu.make_async_copy(rf.at[:, where], rf_hbm.at[:, where], out_sem.at[1, n]),
            ))
            for copy in outs[-1]:
                copy.start()
    for whole, phase in sent:
        pltpu.make_async_copy(whole, whole, send_sem.at[phase]).wait()
    for copies in outs:
        for copy in copies:
            copy.wait()


def body(grads, errors, start_q):
    g, e = grads[0], errors[0]
    rows, columns = g.shape
    tiles = columns // 2 // LANES * 4
    steps = columns // STEP
    hbm, vmem = pl.BlockSpec(memory_space=pl.ANY), pl.BlockSpec(memory_space=pltpu.VMEM)
    right, fresh = pl.pallas_call(
        kernel,
        out_shape=(jax.ShapeDtypeStruct((RANK, columns), F32), jax.ShapeDtypeStruct((rows, columns), BF16)),
        in_specs=[hbm, hbm, vmem],
        out_specs=(hbm, hbm),
        scratch_shapes=[
            pltpu.VMEM((rows, columns), BF16),
            pltpu.VMEM((rows, columns), BF16),
            pltpu.VMEM((rows, columns), BF16),
            pltpu.VMEM((RANK, columns), F32),
            pltpu.VMEM((ITERS, RANK, rows), F32),
            pltpu.VMEM((ITERS, RANK, rows), F32),
            pltpu.VMEM((ITERS, Y, RANK, rows), F32),
            pltpu.VMEM((ITERS, X, 8, LANES), F32),
            pltpu.VMEM((ITERS, 2, tiles, 8, LANES), F32),
            pltpu.VMEM((ITERS, tiles, 8, LANES), F32),
            pltpu.VMEM((ITERS, tiles, 8, LANES), F32),
            pltpu.VMEM((ITERS, PLANE, WINDOW, 8, LANES), F32),
            pltpu.VMEM((ITERS, Z, WINDOW + 1, 8, LANES), F32),
            pltpu.VMEM((ITERS, 2, PLANE, WINDOW, 8, LANES), F32),
            pltpu.SemaphoreType.DMA((2, steps)),
            pltpu.SemaphoreType.DMA((2, steps)),
            pltpu.SemaphoreType.DMA((8 * ITERS,)),
            pltpu.SemaphoreType.DMA((8 * ITERS,)),
        ],
        name="power_iterations",
        compiler_params=pltpu.CompilerParams(collective_id=0, has_side_effects=True, vmem_limit_bytes=48 << 20),
        cost_estimate=pl.CostEstimate(flops=5 * 2 * rows * columns * RANK, bytes_accessed=6 * rows * columns, transcendentals=0),
    )(g, e, start_q.T)
    return right.T, fresh[None]


def solution(mesh):
    return jax.shard_map(
        body,
        mesh=mesh,
        in_specs=(P("dp", "vocab", None), P("dp", "vocab", None), P()),
        out_specs=(P(), P("dp", "vocab", None)),
        check_vma=False,
    )
```

```python
import functools

import jax
import jax.numpy as jnp
from jax import lax
from jax.experimental import pallas as pl
from jax.experimental.pallas import tpu as pltpu
from jax.sharding import PartitionSpec as P

MESH = pl.DeviceIdType.MESH
F32, BF16 = jnp.float32, jnp.bfloat16
ITERS = 2
RANK = 32
LANES = 128
STEP = 768
WINDOW = 5
Y, X, Z = 4, 4, 8
PLANE = Y * X


def split(value):
    high = value.astype(BF16)
    rest = value - high.astype(F32)
    middle = rest.astype(BF16)
    return high, middle, (rest - middle.astype(F32)).astype(BF16)


def dot(a, b, over_a, over_b):
    return lax.dot_general(a, b, (((over_a,), (over_b,)), ((), ())), preferred_element_type=F32)


def lower_inverse(packed):
    row = lax.broadcasted_iota(jnp.int32, (RANK, LANES), 0)
    lane = lax.broadcasted_iota(jnp.int32, (RANK, LANES), 1)
    turned = [packed if r == 1 else pltpu.roll(packed, (RANK - RANK * r) % LANES, 1) for r in range(4)]
    work = jnp.where(lane < RANK, jnp.where(lane == row, 1.0, 0.0), jnp.concatenate(turned, axis=0))
    rows = row[:, :1]
    pivots = jnp.ones((RANK, 1), F32)
    for j in range(RANK):
        column, pivot = work[:, RANK + j : RANK + j + 1], work[j : j + 1, RANK + j : RANK + j + 1]
        factor = jnp.where(rows > j, column / pivot, 0.0)
        pivots = jnp.where(rows == j, pivot, pivots)
        work = work - factor * work[j : j + 1, :]
    return (work * lax.rsqrt(pivots))[:, :RANK]


def six(value):
    high, middle, low = split(value)
    return jnp.concatenate([high, high, high, middle, middle, low], axis=1)


def six_rows(value):
    high, middle, low = split(value)
    return jnp.concatenate([high, middle, low, high, middle, high], axis=0)


def gathered(windows, k):
    parts = []
    for column in range(k * STEP // LANES, (k + 1) * STEP // LANES):
        rows = []
        for r in range(4):
            tile = column * 4 + r
            pair, at = tile // 9, tile % 9
            place, at = (2 * pair, at) if at < WINDOW else (2 * pair + 1, at - WINDOW + 1)
            rows.append(windows[place, at])
        parts.append(jnp.concatenate(rows, axis=0))
    return jnp.concatenate(parts, axis=1)


def finish(windows, k, where, inverse6, basis3, g, e, rf, o):
    right = dot(inverse6, six_rows(gathered(windows, k)), 1, 0)
    rf[:, where] = right
    high, middle, _ = split(right)
    approx = dot(basis3, jnp.concatenate([high, middle, high], axis=0), 1, 0)
    o[:, where] = (g[:, where].astype(F32) + e[:, where].astype(F32) - approx).astype(BF16)


def columns_of(which, k, half):
    return pl.ds(pl.multiple_of(which * half + k * STEP, LANES), STEP)


def last_kernel(rf_in, o_in, g, e, windows, inverse6, basis3, rf_hbm, o_hbm, rf, o, sems):
    c = lax.rem(lax.axis_index("dp"), 2)
    half = g.shape[1] // 2
    copies = []

    def write(src, dst, where):
        copies.append(pltpu.make_async_copy(src.at[:, where], dst.at[:, where], sems.at[len(copies)]))
        copies[-1].start()

    for k in range(half // STEP):
        write(o_in, o_hbm, columns_of(c, k, half))
        write(rf_in, rf_hbm, columns_of(c, k, half))
    for k in range(half // STEP):
        where = columns_of(1 - c, k, half)
        finish(windows, k, where, inverse6[...], basis3[...], g, e, rf, o)
        write(o, o_hbm, where)
        write(rf, rf_hbm, where)
    for copy in copies:
        copy.wait()


def kernel(
    g_hbm, e_hbm, q_hbm, rf, o, g, e, back, inverse_ref, basis_ref,
    q, lp, lr, ly, gx, u, pr, s, rs, zb, ag,
    load_sem, send_sem, recv_sem,
):
    dp, vocab = lax.axis_index("dp"), lax.axis_index("vocab")
    y, c, x, z = dp // 2, lax.rem(dp, 2), vocab // Z, lax.rem(vocab, Z)
    mine = y * X + x
    columns = g.shape[1]
    half = columns // 2
    tiles = half // LANES

    def device(y, c, x, z):
        return (y * 2 + c, x * Z + z)

    sibling = device(y, 1 - c, x, z)
    y_peers = [device(lax.rem(y + k, Y), c, x, z) for k in range(1, Y)]
    x_peers = [device(y, c, lax.rem(x + k, X), z) for k in range(1, X)]
    z_peers = [device(y, c, x, lax.rem(z + k, Z)) for k in range(1, Z)]
    places = [lax.rem(mine + k, PLANE) for k in range(1, PLANE)]
    plane_peers = [device(p // X, c, lax.rem(p, X), z) for p in places]

    loads = []
    for k in range(columns // STEP):
        part = pl.ds(k * STEP, STEP)
        loads.append([
            pltpu.make_async_copy(hbm.at[:, part], vmem.at[:, part], load_sem.at[n, k])
            for n, (hbm, vmem) in enumerate(((q_hbm, q), (g_hbm, g), (e_hbm, e)))
        ])
        for copy in loads[-1]:
            copy.start()

    barrier = pltpu.get_barrier_semaphore()
    everyone = [sibling] + plane_peers + z_peers
    for peer in everyone:
        pl.semaphore_signal(barrier, inc=1, device_id=peer, device_id_type=MESH)

    sent = []

    pending = {}

    def send(src, dst, peers, phase, whole):
        pending[phase] = whole
        sources = src if isinstance(src, list) else [src] * len(peers)
        for source, peer in zip(sources, peers):
            pltpu.make_async_remote_copy(
                src_ref=source, dst_ref=dst, send_sem=send_sem.at[phase], recv_sem=recv_sem.at[phase],
                device_id=peer, device_id_type=MESH,
            ).start()

    def arrive(phase):
        whole = pending.pop(phase)
        pltpu.make_async_copy(whole, whole, recv_sem.at[phase]).wait()
        sent.append((whole, phase))

    def left_part(total, q, where):
        q3 = jnp.concatenate(split(q), axis=0)
        return total + (dot(g[:, where], q3, 1, 1) + dot(e[:, where], q3, 1, 1))

    def right_half(it, l3, which):
        for k in range(half // STEP):
            where = columns_of(which, k, half)
            part = dot(l3, g[:, where], 1, 0) + dot(l3, e[:, where], 1, 0)
            part = part[:RANK] + part[RANK : 2 * RANK] + part[2 * RANK :]
            for n in range(STEP // LANES):
                tile = (k * STEP // LANES + n) * 4
                u[it, which, tile : tile + 4] = part[:, n * LANES : (n + 1) * LANES].reshape(4, 8, LANES)

    total = jnp.zeros((g.shape[0], 3 * RANK), F32)
    inverse = None
    for it in range(ITERS):
        base = 8 * it
        if it == 0:
            for k in range(columns // STEP):
                for copy in loads[k]:
                    copy.wait()
                where = pl.ds(k * STEP, STEP)
                total = left_part(total, q[:, where], where)
            pl.semaphore_wait(barrier, len(everyone))
        else:
            total = jnp.zeros_like(total)
            for k in range(half // STEP):
                total = left_part(total, gathered(ag.at[it - 1], k), columns_of(c, k, half))
            arrive(base - 1)
            for k in range(half // STEP):
                total = left_part(total, gathered(back, k), columns_of(1 - c, k, half))
        turned = jnp.concatenate([total, jnp.zeros((g.shape[0], LANES - 3 * RANK), F32)], axis=1).T
        lp[it] = turned[:RANK] + turned[RANK : 2 * RANK] + turned[2 * RANK : 3 * RANK]
        send(lp.at[it], lr.at[it], [sibling], base, lr.at[it])
        arrive(base)
        ly[it, y] = lp[it] + lr[it]
        send(ly.at[it, y], ly.at[it, y], y_peers, base + 1, ly.at[it, pl.ds(0, Y - 1)])
        arrive(base + 1)
        left = ly[it, 0] + ly[it, 1] + ly[it, 2] + ly[it, 3]
        if it > 0:
            left = dot(six(inverse * 0.125), six_rows(left), 1, 0)

        high, middle, low = split(left)
        other = jnp.concatenate([high, middle, low, high, middle, high], axis=1)
        square = dot(
            jnp.concatenate([high, high, high, middle, middle, low], axis=1),
            jnp.concatenate([other] * 4, axis=0), 1, 1,
        )
        lane = lax.broadcasted_iota(jnp.int32, (8, LANES), 1) // RANK
        packed = square[0:8]
        for r in range(1, 4):
            packed = jnp.where(lane == r, square[8 * r : 8 * r + 8], packed)
        gx[it, x] = packed
        send(gx.at[it, x], gx.at[it, x], x_peers, base + 2, gx.at[it, pl.ds(0, X - 1)])

        l3 = jnp.concatenate([high, middle, low], axis=0)
        right_half(it, l3, 1 - c)
        send(u.at[it, 1 - c], pr.at[it], [sibling], base + 3, pr.at[it])
        right_half(it, l3, c)
        arrive(base + 3)
        s[it] = u[it, c] + pr[it]
        send([s.at[it, pl.ds(9 * p // 2, WINDOW)] for p in places], rs.at[it, mine], plane_peers, base + 4, rs.at[it, pl.ds(0, PLANE - 1)])
        rs[it, mine] = s[it, pl.ds(9 * mine // 2, WINDOW)]
        arrive(base + 2)
        zb[it, z, WINDOW] = gx[it, 0] + gx[it, 1] + gx[it, 2] + gx[it, 3]
        arrive(base + 4)
        piece = rs[it, 0]
        for p in range(1, PLANE):
            piece = piece + rs[it, p]
        zb[it, z, 0:WINDOW] = piece
        send(zb.at[it, z], zb.at[it, z], z_peers, base + 5, zb.at[it, pl.ds(0, Z - 1)])
        arrive(base + 5)
        piece = zb[it, 0]
        for p in range(1, Z):
            piece = piece + zb[it, p]
        ag[it, mine] = piece[:WINDOW]
        send(ag.at[it, mine], ag.at[it, mine], plane_peers, base + 6, ag.at[it, pl.ds(0, PLANE - 1)])
        inverse = lower_inverse(piece[WINDOW])
        arrive(base + 6)
        send(ag.at[it], back, [sibling], base + 7, back)

    last = ITERS - 1
    inverse6 = six(inverse)
    high, middle, _ = split(dot(inverse6, six_rows(left), 1, 0))
    basis3 = jnp.concatenate([high, high, middle], axis=0).astype(F32).T.astype(BF16)
    inverse6 = (inverse6.astype(F32) * 0.125).astype(BF16)
    inverse_ref[...] = inverse6
    basis_ref[...] = basis3
    for k in range(half // STEP):
        finish(ag.at[last], k, columns_of(c, k, half), inverse6, basis3, g, e, rf, o)
    arrive(8 * last + 7)
    for whole, phase in sent:
        pltpu.make_async_copy(whole, whole, send_sem.at[phase]).wait()


def body(grads, errors, start_q):
    g, e = grads[0], errors[0]
    rows, columns = g.shape
    tiles = columns // 2 // LANES * 4
    steps = columns // STEP
    hbm, vmem = pl.BlockSpec(memory_space=pltpu.HBM), pl.BlockSpec(memory_space=pltpu.VMEM)
    held = pl.pallas_call(
        kernel,
        out_shape=(
            pltpu.VMEM((RANK, columns), F32),
            pltpu.VMEM((rows, columns), BF16),
            pltpu.VMEM((rows, columns), BF16),
            pltpu.VMEM((rows, columns), BF16),
            pltpu.VMEM((PLANE, WINDOW, 8, LANES), F32),
            pltpu.VMEM((RANK, 6 * RANK), BF16),
            pltpu.VMEM((rows, 3 * RANK), BF16),
        ),
        in_specs=[hbm] * 3,
        out_specs=(vmem,) * 7,
        scratch_shapes=[
            pltpu.VMEM((RANK, columns), F32),
            pltpu.VMEM((ITERS, RANK, rows), F32),
            pltpu.VMEM((ITERS, RANK, rows), F32),
            pltpu.VMEM((ITERS, Y, RANK, rows), F32),
            pltpu.VMEM((ITERS, X, 8, LANES), F32),
            pltpu.VMEM((ITERS, 2, tiles, 8, LANES), F32),
            pltpu.VMEM((ITERS, tiles, 8, LANES), F32),
            pltpu.VMEM((ITERS, tiles, 8, LANES), F32),
            pltpu.VMEM((ITERS, PLANE, WINDOW, 8, LANES), F32),
            pltpu.VMEM((ITERS, Z, WINDOW + 1, 8, LANES), F32),
            pltpu.VMEM((ITERS, PLANE, WINDOW, 8, LANES), F32),
            pltpu.SemaphoreType.DMA((3, steps)),
            pltpu.SemaphoreType.DMA((8 * ITERS,)),
            pltpu.SemaphoreType.DMA((8 * ITERS,)),
        ],
        name="power_iterations",
        compiler_params=pltpu.CompilerParams(collective_id=0, has_side_effects=True, vmem_limit_bytes=50 << 20),
        cost_estimate=pl.CostEstimate(flops=5 * 2 * rows * columns * RANK, bytes_accessed=6 * rows * columns, transcendentals=0),
    )(g, e, start_q.T)
    right, fresh = pl.pallas_call(
        last_kernel,
        out_shape=(jax.ShapeDtypeStruct((RANK, columns), F32), jax.ShapeDtypeStruct((rows, columns), BF16)),
        in_specs=[vmem] * 7,
        out_specs=(hbm, hbm),
        scratch_shapes=[
            pltpu.VMEM((RANK, columns), F32),
            pltpu.VMEM((rows, columns), BF16),
            pltpu.SemaphoreType.DMA((2 * steps,)),
        ],
        name="other_half",
        compiler_params=pltpu.CompilerParams(vmem_limit_bytes=16 << 20),
        cost_estimate=pl.CostEstimate(flops=2 * rows * columns * RANK, bytes_accessed=3 * rows * columns, transcendentals=0),
    )(*held)
    return right.T, fresh[None]


def solution(mesh):
    return jax.shard_map(
        body,
        mesh=mesh,
        in_specs=(P("dp", "vocab", None), P("dp", "vocab", None), P()),
        out_specs=(P(), P("dp", "vocab", None)),
        check_vma=False,
    )
```

```python
import functools

import jax
import jax.numpy as jnp
from jax import lax
from jax.experimental import pallas as pl
from jax.experimental.pallas import tpu as pltpu
from jax.sharding import PartitionSpec as P

MESH = pl.DeviceIdType.MESH
F32, BF16 = jnp.float32, jnp.bfloat16
ITERS = 2
RANK = 32
LANES = 128
STEP = 768
WINDOW = 5
Y, X, Z = 4, 4, 8
PLANE = Y * X
PHASES = 9


def split(value):
    high = value.astype(BF16)
    rest = value - high.astype(F32)
    middle = rest.astype(BF16)
    return high, middle, (rest - middle.astype(F32)).astype(BF16)


def dot(a, b, over_a, over_b):
    return lax.dot_general(a, b, (((over_a,), (over_b,)), ((), ())), preferred_element_type=F32)


def lower_inverse(packed):
    row = lax.broadcasted_iota(jnp.int32, (RANK, LANES), 0)
    lane = lax.broadcasted_iota(jnp.int32, (RANK, LANES), 1)
    turned = [packed if r == 1 else pltpu.roll(packed, (RANK - RANK * r) % LANES, 1) for r in range(4)]
    work = jnp.where(lane < RANK, jnp.where(lane == row, 1.0, 0.0), jnp.concatenate(turned, axis=0))
    rows = row[:, :1]
    pivots = jnp.ones((RANK, 1), F32)
    for j in range(RANK):
        column, pivot = work[:, RANK + j : RANK + j + 1], work[j : j + 1, RANK + j : RANK + j + 1]
        factor = jnp.where(rows > j, column / pivot, 0.0)
        pivots = jnp.where(rows == j, pivot, pivots)
        work = work - factor * work[j : j + 1, :]
    return (work * lax.rsqrt(pivots))[:, :RANK]


def six(value):
    high, middle, low = split(value)
    return jnp.concatenate([high, high, high, middle, middle, low], axis=1)


def six_rows(value):
    high, middle, low = split(value)
    return jnp.concatenate([high, middle, low, high, middle, high], axis=0)


def gathered(windows, k):
    parts = []
    for column in range(k * STEP // LANES, (k + 1) * STEP // LANES):
        rows = []
        for r in range(4):
            tile = column * 4 + r
            pair, at = tile // 9, tile % 9
            place, at = (2 * pair, at) if at < WINDOW else (2 * pair + 1, at - WINDOW + 1)
            rows.append(windows[place, at])
        parts.append(jnp.concatenate(rows, axis=0))
    return jnp.concatenate(parts, axis=1)


def finish(windows, k, where, inverse6, basis3, g, e, rf, o):
    right = dot(inverse6, six_rows(gathered(windows, k)), 1, 0)
    rf[:, where] = right
    high, middle, _ = split(right)
    approx = dot(basis3, jnp.concatenate([high, middle, high], axis=0), 1, 0)
    o[:, where] = (g[:, where].astype(F32) + e[:, where].astype(F32) - approx).astype(BF16)


def columns_of(which, k, half):
    return pl.ds(pl.multiple_of(which * half + k * STEP, LANES), STEP)


def last_kernel(rf_in, o_in, g, e, windows, inverse6, basis3, rf_hbm, o_hbm, rf, o, sems):
    c = lax.rem(lax.axis_index("dp"), 2)
    half = g.shape[1] // 2
    copies = []

    def write(src, dst, where):
        copies.append(pltpu.make_async_copy(src.at[:, where], dst.at[:, where], sems.at[len(copies)]))
        copies[-1].start()

    for k in range(half // STEP):
        write(o_in, o_hbm, columns_of(c, k, half))
        write(rf_in, rf_hbm, columns_of(c, k, half))
    for k in range(half // STEP):
        where = columns_of(1 - c, k, half)
        finish(windows, k, where, inverse6[...], basis3[...], g, e, rf, o)
        write(o, o_hbm, where)
        write(rf, rf_hbm, where)
    for copy in copies:
        copy.wait()


def kernel(
    g_hbm, e_hbm, q_hbm, rf, o, g, e, back, inverse_ref, basis_ref,
    q, lp, lr, ly, gx, gz, u, pr, s, rs, zb, ag,
    load_sem, send_sem, recv_sem,
):
    dp, vocab = lax.axis_index("dp"), lax.axis_index("vocab")
    y, c, x, z = dp // 2, lax.rem(dp, 2), vocab // Z, lax.rem(vocab, Z)
    mine = y * X + x
    columns = g.shape[1]
    half = columns // 2
    tiles = half // LANES

    def device(y, c, x, z):
        return (y * 2 + c, x * Z + z)

    sibling = device(y, 1 - c, x, z)
    y_peers = [device(lax.rem(y + k, Y), c, x, z) for k in (2, 1, 3)]
    x_peers = [device(y, c, lax.rem(x + k, X), z) for k in (2, 1, 3)]
    far = lambda k, size: min(k, size - k)
    z_peers = [device(y, c, x, lax.rem(z + k, Z)) for k in sorted(range(1, Z), key=lambda k: -far(k, Z))]
    steps = [(j, k) for j in range(Y) for k in range(X) if j + k > 0]
    steps.sort(key=lambda jk: -far(jk[0], Y) - far(jk[1], X))
    across = [(lax.rem(y + j, Y), lax.rem(x + k, X)) for j, k in steps]
    places = [j * X + k for j, k in across]
    plane_peers = [device(j, c, k, z) for j, k in across]

    loads = []
    for k in range(columns // STEP):
        part = pl.ds(k * STEP, STEP)
        loads.append([
            pltpu.make_async_copy(hbm.at[:, part], vmem.at[:, part], load_sem.at[n, k])
            for n, (hbm, vmem) in enumerate(((q_hbm, q), (g_hbm, g), (e_hbm, e)))
        ])
        for copy in loads[-1]:
            copy.start()

    barrier = pltpu.get_barrier_semaphore()
    everyone = [sibling] + plane_peers + z_peers
    for peer in everyone:
        pl.semaphore_signal(barrier, inc=1, device_id=peer, device_id_type=MESH)

    sent = []

    pending = {}

    def send(src, dst, peers, phase, whole):
        pending[phase] = whole
        sources = src if isinstance(src, list) else [src] * len(peers)
        for source, peer in zip(sources, peers):
            pltpu.make_async_remote_copy(
                src_ref=source, dst_ref=dst, send_sem=send_sem.at[phase], recv_sem=recv_sem.at[phase],
                device_id=peer, device_id_type=MESH,
            ).start()

    def arrive(phase):
        whole = pending.pop(phase)
        pltpu.make_async_copy(whole, whole, recv_sem.at[phase]).wait()
        sent.append((whole, phase))

    def left_part(total, q, where):
        q3 = jnp.concatenate(split(q), axis=0)
        return total + (dot(g[:, where], q3, 1, 1) + dot(e[:, where], q3, 1, 1))

    def right_half(it, l3, which, send_it):
        for k in range(half // STEP):
            where = columns_of(which, k, half)
            part = dot(l3, g[:, where], 1, 0) + dot(l3, e[:, where], 1, 0)
            part = part[:RANK] + part[RANK : 2 * RANK] + part[2 * RANK :]
            for n in range(STEP // LANES):
                tile = (k * STEP // LANES + n) * 4
                u[it, which, tile : tile + 4] = part[:, n * LANES : (n + 1) * LANES].reshape(4, 8, LANES)
            if send_it:
                span = pl.ds(k * STEP // LANES * 4, STEP // LANES * 4)
                send(u.at[it, which, span], pr.at[it, span], [sibling], PHASES * it + 3, pr.at[it])

    total = jnp.zeros((g.shape[0], 3 * RANK), F32)
    inverse = None
    for it in range(ITERS):
        base = PHASES * it
        if it == 0:
            for k in range(columns // STEP):
                for copy in loads[k]:
                    copy.wait()
                where = pl.ds(k * STEP, STEP)
                total = left_part(total, q[:, where], where)
            pl.semaphore_wait(barrier, len(everyone))
        else:
            total = jnp.zeros_like(total)
            for k in range(half // STEP):
                total = left_part(total, gathered(ag.at[it - 1], k), columns_of(c, k, half))
            arrive(base - PHASES + 7)
            for k in range(half // STEP):
                total = left_part(total, gathered(back, k), columns_of(1 - c, k, half))
        turned = jnp.concatenate([total, jnp.zeros((g.shape[0], LANES - 3 * RANK), F32)], axis=1).T
        lp[it] = turned[:RANK] + turned[RANK : 2 * RANK] + turned[2 * RANK : 3 * RANK]
        send(lp.at[it], lr.at[it], [sibling], base, lr.at[it])
        arrive(base)
        ly[it, y] = lp[it] + lr[it]
        send(ly.at[it, y], ly.at[it, y], y_peers, base + 1, ly.at[it, pl.ds(0, Y - 1)])
        arrive(base + 1)
        left = ly[it, 0] + ly[it, 1] + ly[it, 2] + ly[it, 3]
        if it > 0:
            left = dot(six(inverse * 0.125), six_rows(left), 1, 0)

        high, middle, low = split(left)
        l3 = jnp.concatenate([high, middle, low], axis=0)
        right_half(it, l3, 1 - c, True)

        other = jnp.concatenate([high, middle, low, high, middle, high], axis=1)
        square = dot(
            jnp.concatenate([high, high, high, middle, middle, low], axis=1),
            jnp.concatenate([other] * 4, axis=0), 1, 1,
        )
        lane = lax.broadcasted_iota(jnp.int32, (8, LANES), 1) // RANK
        packed = square[0:8]
        for r in range(1, 4):
            packed = jnp.where(lane == r, square[8 * r : 8 * r + 8], packed)
        gx[it, x] = packed
        send(gx.at[it, x], gx.at[it, x], x_peers, base + 2, gx.at[it, pl.ds(0, X - 1)])

        right_half(it, l3, c, False)
        arrive(base + 3)

        s[it] = u[it, c] + pr[it]
        send([s.at[it, pl.ds(9 * p // 2, WINDOW)] for p in places], rs.at[it, mine], plane_peers, base + 4, rs.at[it, pl.ds(0, PLANE - 1)])
        rs[it, mine] = s[it, pl.ds(9 * mine // 2, WINDOW)]
        arrive(base + 2)
        gz[it, z] = gx[it, 0] + gx[it, 1] + gx[it, 2] + gx[it, 3]
        send(gz.at[it, z], gz.at[it, z], z_peers, base + 8, gz.at[it, pl.ds(0, Z - 1)])
        arrive(base + 4)
        piece = rs[it, 0]
        for p in range(1, PLANE):
            piece = piece + rs[it, p]
        zb[it, z] = piece
        send(zb.at[it, z], zb.at[it, z], z_peers, base + 5, zb.at[it, pl.ds(0, Z - 1)])
        arrive(base + 8)
        gram = gz[it, 0]
        for p in range(1, Z):
            gram = gram + gz[it, p]
        inverse = lower_inverse(gram)
        arrive(base + 5)
        piece = zb[it, 0]
        for p in range(1, Z):
            piece = piece + zb[it, p]
        ag[it, mine] = piece
        send(ag.at[it, mine], ag.at[it, mine], plane_peers, base + 6, ag.at[it, pl.ds(0, PLANE - 1)])
        arrive(base + 6)
        send(ag.at[it], back, [sibling], base + 7, back)

    last = ITERS - 1
    inverse6 = six(inverse)
    high, middle, _ = split(dot(inverse6, six_rows(left), 1, 0))
    basis3 = jnp.concatenate([high, high, middle], axis=0).astype(F32).T.astype(BF16)
    inverse6 = (inverse6.astype(F32) * 0.125).astype(BF16)
    inverse_ref[...] = inverse6
    basis_ref[...] = basis3
    for k in range(half // STEP):
        finish(ag.at[last], k, columns_of(c, k, half), inverse6, basis3, g, e, rf, o)
    arrive(PHASES * last + 7)
    for whole, phase in sent:
        pltpu.make_async_copy(whole, whole, send_sem.at[phase]).wait()


def body(grads, errors, start_q):
    g, e = grads[0], errors[0]
    rows, columns = g.shape
    tiles = columns // 2 // LANES * 4
    steps = columns // STEP
    hbm, vmem = pl.BlockSpec(memory_space=pltpu.HBM), pl.BlockSpec(memory_space=pltpu.VMEM)
    held = pl.pallas_call(
        kernel,
        out_shape=(
            pltpu.VMEM((RANK, columns), F32),
            pltpu.VMEM((rows, columns), BF16),
            pltpu.VMEM((rows, columns), BF16),
            pltpu.VMEM((rows, columns), BF16),
            pltpu.VMEM((PLANE, WINDOW, 8, LANES), F32),
            pltpu.VMEM((RANK, 6 * RANK), BF16),
            pltpu.VMEM((rows, 3 * RANK), BF16),
        ),
        in_specs=[hbm] * 3,
        out_specs=(vmem,) * 7,
        scratch_shapes=[
            pltpu.VMEM((RANK, columns), F32),
            pltpu.VMEM((ITERS, RANK, rows), F32),
            pltpu.VMEM((ITERS, RANK, rows), F32),
            pltpu.VMEM((ITERS, Y, RANK, rows), F32),
            pltpu.VMEM((ITERS, X, 8, LANES), F32),
            pltpu.VMEM((ITERS, Z, 8, LANES), F32),
            pltpu.VMEM((ITERS, 2, tiles, 8, LANES), F32),
            pltpu.VMEM((ITERS, tiles, 8, LANES), F32),
            pltpu.VMEM((ITERS, tiles, 8, LANES), F32),
            pltpu.VMEM((ITERS, PLANE, WINDOW, 8, LANES), F32),
            pltpu.VMEM((ITERS, Z, WINDOW, 8, LANES), F32),
            pltpu.VMEM((ITERS, PLANE, WINDOW, 8, LANES), F32),
            pltpu.SemaphoreType.DMA((3, steps)),
            pltpu.SemaphoreType.DMA((PHASES * ITERS,)),
            pltpu.SemaphoreType.DMA((PHASES * ITERS,)),
        ],
        name="power_iterations",
        compiler_params=pltpu.CompilerParams(collective_id=0, has_side_effects=True, vmem_limit_bytes=50 << 20),
        cost_estimate=pl.CostEstimate(flops=5 * 2 * rows * columns * RANK, bytes_accessed=6 * rows * columns, transcendentals=0),
    )(g, e, start_q.T)
    right, fresh = pl.pallas_call(
        last_kernel,
        out_shape=(jax.ShapeDtypeStruct((RANK, columns), F32), jax.ShapeDtypeStruct((rows, columns), BF16)),
        in_specs=[vmem] * 7,
        out_specs=(hbm, hbm),
        scratch_shapes=[
            pltpu.VMEM((RANK, columns), F32),
            pltpu.VMEM((rows, columns), BF16),
            pltpu.SemaphoreType.DMA((2 * steps,)),
        ],
        name="other_half",
        compiler_params=pltpu.CompilerParams(vmem_limit_bytes=16 << 20),
        cost_estimate=pl.CostEstimate(flops=2 * rows * columns * RANK, bytes_accessed=3 * rows * columns, transcendentals=0),
    )(*held)
    return right.T, fresh[None]


def solution(mesh):
    return jax.shard_map(
        body,
        mesh=mesh,
        in_specs=(P("dp", "vocab", None), P("dp", "vocab", None), P()),
        out_specs=(P(), P("dp", "vocab", None)),
        check_vma=False,
    )
```

```python
import functools

import jax
import jax.numpy as jnp
from jax import lax
from jax.experimental import pallas as pl
from jax.experimental.pallas import tpu as pltpu
from jax.sharding import PartitionSpec as P

MESH = pl.DeviceIdType.MESH
F32, BF16 = jnp.float32, jnp.bfloat16
ITERS = 2
RANK = 32
LANES = 128
STEP = 768
WINDOW = 5
Y, X, Z = 4, 4, 8
PLANE = Y * X
PHASES = 9
BULK = PHASES * ITERS


def split(value):
    high = value.astype(BF16)
    rest = value - high.astype(F32)
    middle = rest.astype(BF16)
    return high, middle, (rest - middle.astype(F32)).astype(BF16)


def dot(a, b, over_a, over_b):
    return lax.dot_general(a, b, (((over_a,), (over_b,)), ((), ())), preferred_element_type=F32)


def lower_inverse(packed):
    row = lax.broadcasted_iota(jnp.int32, (RANK, LANES), 0)
    lane = lax.broadcasted_iota(jnp.int32, (RANK, LANES), 1)
    turned = [packed if r == 1 else pltpu.roll(packed, (RANK - RANK * r) % LANES, 1) for r in range(4)]
    work = jnp.where(lane < RANK, jnp.where(lane == row, 1.0, 0.0), jnp.concatenate(turned, axis=0))
    rows = row[:, :1]
    pivots = jnp.ones((RANK, 1), F32)
    for j in range(RANK):
        column, pivot = work[:, RANK + j : RANK + j + 1], work[j : j + 1, RANK + j : RANK + j + 1]
        factor = jnp.where(rows > j, column / pivot, 0.0)
        pivots = jnp.where(rows == j, pivot, pivots)
        work = work - factor * work[j : j + 1, :]
    return (work * lax.rsqrt(pivots))[:, :RANK]


def six(value):
    high, middle, low = split(value)
    return jnp.concatenate([high, high, high, middle, middle, low], axis=1)


def six_rows(value):
    high, middle, low = split(value)
    return jnp.concatenate([high, middle, low, high, middle, high], axis=0)


def gathered(windows, k):
    parts = []
    for column in range(k * STEP // LANES, (k + 1) * STEP // LANES):
        rows = []
        for r in range(4):
            tile = column * 4 + r
            pair, at = tile // 9, tile % 9
            place, at = (2 * pair, at) if at < WINDOW else (2 * pair + 1, at - WINDOW + 1)
            rows.append(windows[place, at])
        parts.append(jnp.concatenate(rows, axis=0))
    return jnp.concatenate(parts, axis=1)


def finish(windows, k, where, inverse6, basis3, g, e, rf, o):
    right = dot(inverse6, six_rows(gathered(windows, k)), 1, 0)
    rf[:, where] = right
    high, middle, _ = split(right)
    approx = dot(basis3, jnp.concatenate([high, middle, high], axis=0), 1, 0)
    o[:, where] = (g[:, where].astype(F32) + e[:, where].astype(F32) - approx).astype(BF16)


def columns_of(which, k, half):
    return pl.ds(pl.multiple_of(which * half + k * STEP, LANES), STEP)


def last_kernel(rf_in, o_in, g, e, windows, inverse6, basis3, rf_hbm, o_hbm, rf, o, sems):
    c = lax.rem(lax.axis_index("dp"), 2)
    half = g.shape[1] // 2
    copies = []

    def write(src, dst, where):
        copies.append(pltpu.make_async_copy(src.at[:, where], dst.at[:, where], sems.at[len(copies)]))
        copies[-1].start()

    for k in range(half // STEP):
        write(o_in, o_hbm, columns_of(c, k, half))
        write(rf_in, rf_hbm, columns_of(c, k, half))
    for k in range(half // STEP):
        where = columns_of(1 - c, k, half)
        finish(windows, k, where, inverse6[...], basis3[...], g, e, rf, o)
        write(o, o_hbm, where)
        write(rf, rf_hbm, where)
    for copy in copies:
        copy.wait()


def kernel(
    g_hbm, e_hbm, q_hbm, rf, o, g, e, back, inverse_ref, basis_ref,
    q, lp, lr, ly, gx, gz, s, rs, zb, ag, mixed, mixed_in, m3,
    load_sem, send_sem, recv_sem,
):
    dp, vocab = lax.axis_index("dp"), lax.axis_index("vocab")
    y, c, x, z = dp // 2, lax.rem(dp, 2), vocab // Z, lax.rem(vocab, Z)
    mine = y * X + x
    columns = g.shape[1]
    half = columns // 2
    tiles = half // LANES

    def device(y, c, x, z):
        return (y * 2 + c, x * Z + z)

    sibling = device(y, 1 - c, x, z)
    y_peers = [device(lax.rem(y + k, Y), c, x, z) for k in (2, 1, 3)]
    x_peers = [device(y, c, lax.rem(x + k, X), z) for k in (2, 1, 3)]
    far = lambda k, size: min(k, size - k)
    z_peers = [device(y, c, x, lax.rem(z + k, Z)) for k in sorted(range(1, Z), key=lambda k: -far(k, Z))]
    steps = [(j, k) for j in range(Y) for k in range(X) if j + k > 0]
    steps.sort(key=lambda jk: -far(jk[0], Y) - far(jk[1], X))
    across = [(lax.rem(y + j, Y), lax.rem(x + k, X)) for j, k in steps]
    places = [j * X + k for j, k in across]
    plane_peers = [device(j, c, k, z) for j, k in across]

    chunks = [(which, k, columns_of(which, k, half)) for which in (1 - c, c) for k in range(half // STEP)]
    loads = []
    for n, (which, k, part) in enumerate(chunks):
        loads.append([
            pltpu.make_async_copy(hbm.at[:, part], vmem.at[:, part], load_sem.at[m, n])
            for m, (hbm, vmem) in enumerate(((q_hbm, q), (g_hbm, g), (e_hbm, e)))
        ])
        for copy in loads[-1]:
            copy.start()

    barrier = pltpu.get_barrier_semaphore()
    everyone = [sibling] + plane_peers + z_peers
    for peer in everyone:
        pl.semaphore_signal(barrier, inc=1, device_id=peer, device_id_type=MESH)

    sent = []

    pending = {}

    def send(src, dst, peers, phase, whole):
        pending[phase] = whole
        sources = src if isinstance(src, list) else [src] * len(peers)
        for source, peer in zip(sources, peers):
            pltpu.make_async_remote_copy(
                src_ref=source, dst_ref=dst, send_sem=send_sem.at[phase], recv_sem=recv_sem.at[phase],
                device_id=peer, device_id_type=MESH,
            ).start()

    def arrive(phase):
        whole = pending.pop(phase)
        pltpu.make_async_copy(whole, whole, recv_sem.at[phase]).wait()
        sent.append((whole, phase))

    def split3(q):
        return jnp.concatenate(split(q), axis=0)

    size = g.shape[0]
    inverse = None
    for it in range(ITERS):
        base = PHASES * it
        total = jnp.zeros((size, 3 * RANK), F32)
        if it == 0:
            for copies, (which, k, where) in zip(loads, chunks):
                for copy in copies:
                    copy.wait()
                q3 = split3(q[:, where])
                total = total + (dot(g[:, where], q3, 1, 1) + dot(e[:, where], q3, 1, 1))
            pl.semaphore_wait(barrier, len(everyone))
        else:
            for k in range(half // STEP):
                part = dot(m3[:, k * STEP : (k + 1) * STEP], split3(gathered(ag.at[it - 1], k)), 1, 1)
                total = total + (part[:size] + part[size : 2 * size] + part[2 * size :])
        turned = jnp.concatenate([total, jnp.zeros((size, LANES - 3 * RANK), F32)], axis=1).T
        lp[it] = turned[:RANK] + turned[RANK : 2 * RANK] + turned[2 * RANK : 3 * RANK]
        send(lp.at[it], lr.at[it], [sibling], base, lr.at[it])
        if it == 0:
            for k in range(half // STEP):
                where = columns_of(1 - c, k, half)
                mixed[k] = g[:, where].astype(F32) + e[:, where].astype(F32)
        arrive(base)
        ly[it, y] = lp[it] + lr[it]
        send(ly.at[it, y], ly.at[it, y], y_peers, base + 1, ly.at[it, pl.ds(0, Y - 1)])
        if it == 0:
            for k in range(half // STEP):
                send(mixed.at[k], mixed_in.at[k], [sibling], BULK + k, mixed_in.at[k])
        if it == 0:
            for k in range(half // STEP):
                where = columns_of(c, k, half)
                here = g[:, where].astype(F32) + e[:, where].astype(F32)
                arrive(BULK + k)
                for n, part in enumerate(split(here + mixed_in[k])):
                    m3[n * size : (n + 1) * size, k * STEP : (k + 1) * STEP] = part
        arrive(base + 1)
        left = ly[it, 0] + ly[it, 1] + ly[it, 2] + ly[it, 3]
        if it > 0:
            left = dot(six(inverse * 0.125), six_rows(left), 1, 0)

        high, middle, low = split(left)
        l9 = jnp.concatenate([jnp.concatenate([high, middle, low], axis=0)] * 3, axis=1)
        for k in range(half // STEP):
            part = dot(l9, m3[:, k * STEP : (k + 1) * STEP], 1, 0)
            part = part[:RANK] + part[RANK : 2 * RANK] + part[2 * RANK :]
            for n in range(STEP // LANES):
                tile = (k * STEP // LANES + n) * 4
                s[it, tile : tile + 4] = part[:, n * LANES : (n + 1) * LANES].reshape(4, 8, LANES)
        send([s.at[it, pl.ds(9 * p // 2, WINDOW)] for p in places], rs.at[it, mine], plane_peers, base + 4, rs.at[it, pl.ds(0, PLANE - 1)])

        other = jnp.concatenate([high, middle, low, high, middle, high], axis=1)
        square = dot(
            jnp.concatenate([high, high, high, middle, middle, low], axis=1),
            jnp.concatenate([other] * 4, axis=0), 1, 1,
        )
        lane = lax.broadcasted_iota(jnp.int32, (8, LANES), 1) // RANK
        packed = square[0:8]
        for r in range(1, 4):
            packed = jnp.where(lane == r, square[8 * r : 8 * r + 8], packed)
        gx[it, x] = packed
        send(gx.at[it, x], gx.at[it, x], x_peers, base + 2, gx.at[it, pl.ds(0, X - 1)])

        rs[it, mine] = s[it, pl.ds(9 * mine // 2, WINDOW)]
        arrive(base + 4)
        piece = rs[it, 0]
        for p in range(1, PLANE):
            piece = piece + rs[it, p]
        zb[it, z] = piece
        send(zb.at[it, z], zb.at[it, z], z_peers, base + 5, zb.at[it, pl.ds(0, Z - 1)])
        arrive(base + 2)
        gz[it, z] = gx[it, 0] + gx[it, 1] + gx[it, 2] + gx[it, 3]
        send(gz.at[it, z], gz.at[it, z], z_peers, base + 8, gz.at[it, pl.ds(0, Z - 1)])
        arrive(base + 5)
        piece = zb[it, 0]
        for p in range(1, Z):
            piece = piece + zb[it, p]
        ag[it, mine] = piece
        send(ag.at[it, mine], ag.at[it, mine], plane_peers, base + 6, ag.at[it, pl.ds(0, PLANE - 1)])
        arrive(base + 8)
        gram = gz[it, 0]
        for p in range(1, Z):
            gram = gram + gz[it, p]
        inverse = lower_inverse(gram)
        arrive(base + 6)
    send(ag.at[ITERS - 1], back, [sibling], PHASES * ITERS - 2, back)

    last = ITERS - 1
    inverse6 = six(inverse)
    high, middle, _ = split(dot(inverse6, six_rows(left), 1, 0))
    basis3 = jnp.concatenate([high, high, middle], axis=0).astype(F32).T.astype(BF16)
    inverse6 = (inverse6.astype(F32) * 0.125).astype(BF16)
    inverse_ref[...] = inverse6
    basis_ref[...] = basis3
    for k in range(half // STEP):
        finish(ag.at[last], k, columns_of(c, k, half), inverse6, basis3, g, e, rf, o)
    arrive(PHASES * ITERS - 2)
    for whole, phase in sent:
        pltpu.make_async_copy(whole, whole, send_sem.at[phase]).wait()


def body(grads, errors, start_q):
    g, e = grads[0], errors[0]
    rows, columns = g.shape
    tiles = columns // 2 // LANES * 4
    steps = columns // STEP
    hbm, vmem = pl.BlockSpec(memory_space=pltpu.HBM), pl.BlockSpec(memory_space=pltpu.VMEM)
    held = pl.pallas_call(
        kernel,
        out_shape=(
            pltpu.VMEM((RANK, columns), F32),
            pltpu.VMEM((rows, columns), BF16),
            pltpu.VMEM((rows, columns), BF16),
            pltpu.VMEM((rows, columns), BF16),
            pltpu.VMEM((PLANE, WINDOW, 8, LANES), F32),
            pltpu.VMEM((RANK, 6 * RANK), BF16),
            pltpu.VMEM((rows, 3 * RANK), BF16),
        ),
        in_specs=[hbm] * 3,
        out_specs=(vmem,) * 7,
        scratch_shapes=[
            pltpu.VMEM((RANK, columns), F32),
            pltpu.VMEM((ITERS, RANK, rows), F32),
            pltpu.VMEM((ITERS, RANK, rows), F32),
            pltpu.VMEM((ITERS, Y, RANK, rows), F32),
            pltpu.VMEM((ITERS, X, 8, LANES), F32),
            pltpu.VMEM((ITERS, Z, 8, LANES), F32),
            pltpu.VMEM((ITERS, tiles, 8, LANES), F32),
            pltpu.VMEM((ITERS, PLANE, WINDOW, 8, LANES), F32),
            pltpu.VMEM((ITERS, Z, WINDOW, 8, LANES), F32),
            pltpu.VMEM((ITERS, PLANE, WINDOW, 8, LANES), F32),
            pltpu.VMEM((steps // 2, rows, STEP), F32),
            pltpu.VMEM((steps // 2, rows, STEP), F32),
            pltpu.VMEM((3 * rows, columns // 2), BF16),
            pltpu.SemaphoreType.DMA((3, steps)),
            pltpu.SemaphoreType.DMA((PHASES * ITERS + steps // 2,)),
            pltpu.SemaphoreType.DMA((PHASES * ITERS + steps // 2,)),
        ],
        name="power_iterations",
        compiler_params=pltpu.CompilerParams(collective_id=0, has_side_effects=True, vmem_limit_bytes=50 << 20),
        cost_estimate=pl.CostEstimate(flops=5 * 2 * rows * columns * RANK, bytes_accessed=6 * rows * columns, transcendentals=0),
    )(g, e, start_q.T)
    right, fresh = pl.pallas_call(
        last_kernel,
        out_shape=(jax.ShapeDtypeStruct((RANK, columns), F32), jax.ShapeDtypeStruct((rows, columns), BF16)),
        in_specs=[vmem] * 7,
        out_specs=(hbm, hbm),
        scratch_shapes=[
            pltpu.VMEM((RANK, columns), F32),
            pltpu.VMEM((rows, columns), BF16),
            pltpu.SemaphoreType.DMA((2 * steps,)),
        ],
        name="other_half",
        compiler_params=pltpu.CompilerParams(vmem_limit_bytes=16 << 20),
        cost_estimate=pl.CostEstimate(flops=2 * rows * columns * RANK, bytes_accessed=3 * rows * columns, transcendentals=0),
    )(*held)
    return right.T, fresh[None]


def solution(mesh):
    return jax.shard_map(
        body,
        mesh=mesh,
        in_specs=(P("dp", "vocab", None), P("dp", "vocab", None), P()),
        out_specs=(P(), P("dp", "vocab", None)),
        check_vma=False,
    )
```

```python
import functools

import jax
import jax.numpy as jnp
from jax import lax
from jax.experimental import pallas as pl
from jax.experimental.pallas import tpu as pltpu
from jax.sharding import PartitionSpec as P

MESH = pl.DeviceIdType.MESH
F32, BF16 = jnp.float32, jnp.bfloat16
ITERS = 2
RANK = 32
LANES = 128
STEP = 768
WINDOW = 5
Y, X, Z = 4, 4, 8
PLANE = Y * X
PARTS = (2, 2, 1)
PHASES = 15
BULK = PHASES * ITERS


def split(value):
    high = value.astype(BF16)
    rest = value - high.astype(F32)
    middle = rest.astype(BF16)
    return high, middle, (rest - middle.astype(F32)).astype(BF16)


def dot(a, b, over_a, over_b):
    return lax.dot_general(a, b, (((over_a,), (over_b,)), ((), ())), preferred_element_type=F32)


def lower_inverse(packed):
    row = lax.broadcasted_iota(jnp.int32, (RANK, LANES), 0)
    lane = lax.broadcasted_iota(jnp.int32, (RANK, LANES), 1)
    turned = [packed if r == 1 else pltpu.roll(packed, (RANK - RANK * r) % LANES, 1) for r in range(4)]
    work = jnp.where(lane < RANK, jnp.where(lane == row, 1.0, 0.0), jnp.concatenate(turned, axis=0))
    rows = row[:, :1]
    pivots = jnp.ones((RANK, 1), F32)
    for j in range(RANK):
        column, pivot = work[:, RANK + j : RANK + j + 1], work[j : j + 1, RANK + j : RANK + j + 1]
        factor = jnp.where(rows > j, column / pivot, 0.0)
        pivots = jnp.where(rows == j, pivot, pivots)
        work = work - factor * work[j : j + 1, :]
    return (work * lax.rsqrt(pivots))[:, :RANK]


def six(value):
    high, middle, low = split(value)
    return jnp.concatenate([high, high, high, middle, middle, low], axis=1)


def six_rows(value):
    high, middle, low = split(value)
    return jnp.concatenate([high, middle, low, high, middle, high], axis=0)


def gathered(windows, k):
    parts = []
    for column in range(k * STEP // LANES, (k + 1) * STEP // LANES):
        rows = []
        for r in range(4):
            tile = column * 4 + r
            pair, at = tile // 9, tile % 9
            place, at = (2 * pair, at) if at < WINDOW else (2 * pair + 1, at - WINDOW + 1)
            rows.append(windows[place, at])
        parts.append(jnp.concatenate(rows, axis=0))
    return jnp.concatenate(parts, axis=1)


def finish(windows, k, where, inverse6, basis3, g, e, rf, o):
    right = dot(inverse6, six_rows(gathered(windows, k)), 1, 0)
    rf[:, where] = right
    high, middle, _ = split(right)
    approx = dot(basis3, jnp.concatenate([high, middle, high], axis=0), 1, 0)
    o[:, where] = (g[:, where].astype(F32) + e[:, where].astype(F32) - approx).astype(BF16)


def columns_of(which, k, half):
    return pl.ds(pl.multiple_of(which * half + k * STEP, LANES), STEP)


def last_kernel(rf_in, o_in, g, e, windows, inverse6, basis3, rf_hbm, o_hbm, rf, o, sems):
    c = lax.rem(lax.axis_index("dp"), 2)
    half = g.shape[1] // 2
    copies = []

    def write(src, dst, where):
        copies.append(pltpu.make_async_copy(src.at[:, where], dst.at[:, where], sems.at[len(copies)]))
        copies[-1].start()

    for k in range(half // STEP):
        write(o_in, o_hbm, columns_of(c, k, half))
        write(rf_in, rf_hbm, columns_of(c, k, half))
    for k in range(half // STEP):
        where = columns_of(1 - c, k, half)
        finish(windows, k, where, inverse6[...], basis3[...], g, e, rf, o)
        write(o, o_hbm, where)
        write(rf, rf_hbm, where)
    for copy in copies:
        copy.wait()


def kernel(
    g_hbm, e_hbm, q_hbm, rf, o, g, e, back, inverse_ref, basis_ref,
    q, lp, lr, ly, gx, gz, s, rs, zb, ag, mixed, mixed_in, m3,
    load_sem, send_sem, recv_sem,
):
    dp, vocab = lax.axis_index("dp"), lax.axis_index("vocab")
    y, c, x, z = dp // 2, lax.rem(dp, 2), vocab // Z, lax.rem(vocab, Z)
    mine = y * X + x
    columns = g.shape[1]
    half = columns // 2
    tiles = half // LANES

    def device(y, c, x, z):
        return (y * 2 + c, x * Z + z)

    sibling = device(y, 1 - c, x, z)
    y_peers = [device(lax.rem(y + k, Y), c, x, z) for k in (2, 1, 3)]
    x_peers = [device(y, c, lax.rem(x + k, X), z) for k in (2, 1, 3)]
    far = lambda k, size: min(k, size - k)
    z_peers = [device(y, c, x, lax.rem(z + k, Z)) for k in sorted(range(1, Z), key=lambda k: -far(k, Z))]
    steps = [(j, k) for j in range(Y) for k in range(X) if j + k > 0]
    steps.sort(key=lambda jk: -far(jk[0], Y) - far(jk[1], X))
    across = [(lax.rem(y + j, Y), lax.rem(x + k, X)) for j, k in steps]
    places = [j * X + k for j, k in across]
    plane_peers = [device(j, c, k, z) for j, k in across]

    chunks = [(which, k, columns_of(which, k, half)) for which in (1 - c, c) for k in range(half // STEP)]
    loads = []
    for n, (which, k, part) in enumerate(chunks):
        loads.append([
            pltpu.make_async_copy(hbm.at[:, part], vmem.at[:, part], load_sem.at[m, n])
            for m, (hbm, vmem) in enumerate(((q_hbm, q), (g_hbm, g), (e_hbm, e)))
        ])
        for copy in loads[-1]:
            copy.start()

    barrier = pltpu.get_barrier_semaphore()
    everyone = [sibling] + plane_peers + z_peers
    for peer in everyone:
        pl.semaphore_signal(barrier, inc=1, device_id=peer, device_id_type=MESH)

    sent = []

    pending = {}

    def send(src, dst, peers, phase, whole):
        pending[phase] = whole
        sources = src if isinstance(src, list) else [src] * len(peers)
        for source, peer in zip(sources, peers):
            pltpu.make_async_remote_copy(
                src_ref=source, dst_ref=dst, send_sem=send_sem.at[phase], recv_sem=recv_sem.at[phase],
                device_id=peer, device_id_type=MESH,
            ).start()

    def arrive(phase):
        whole = pending.pop(phase)
        pltpu.make_async_copy(whole, whole, recv_sem.at[phase]).wait()
        sent.append((whole, phase))

    def split3(q):
        return jnp.concatenate(split(q), axis=0)

    size = g.shape[0]
    inverse = None
    for it in range(ITERS):
        base = PHASES * it
        total = jnp.zeros((size, 3 * RANK), F32)
        if it == 0:
            for copies, (which, k, where) in zip(loads, chunks):
                for copy in copies:
                    copy.wait()
                q3 = split3(q[:, where])
                total = total + (dot(g[:, where], q3, 1, 1) + dot(e[:, where], q3, 1, 1))
            pl.semaphore_wait(barrier, len(everyone))
        else:
            for k in range(half // STEP):
                part = dot(m3[:, k * STEP : (k + 1) * STEP], split3(gathered(ag.at[it - 1], k)), 1, 1)
                total = total + (part[:size] + part[size : 2 * size] + part[2 * size :])
        turned = jnp.concatenate([total, jnp.zeros((size, LANES - 3 * RANK), F32)], axis=1).T
        lp[it] = turned[:RANK] + turned[RANK : 2 * RANK] + turned[2 * RANK : 3 * RANK]
        send(lp.at[it], lr.at[it], [sibling], base, lr.at[it])
        if it == 0:
            for k in range(half // STEP):
                where = columns_of(1 - c, k, half)
                mixed[k] = g[:, where].astype(F32) + e[:, where].astype(F32)
                send(mixed.at[k], mixed_in.at[k], [sibling], BULK + k, mixed_in.at[k])
        arrive(base)
        ly[it, y] = lp[it] + lr[it]
        send(ly.at[it, y], ly.at[it, y], y_peers, base + 1, ly.at[it, pl.ds(0, Y - 1)])
        if it == 0:
            for k in range(half // STEP):
                where = columns_of(c, k, half)
                here = g[:, where].astype(F32) + e[:, where].astype(F32)
                arrive(BULK + k)
                for n, part in enumerate(split(here + mixed_in[k])):
                    m3[n * size : (n + 1) * size, k * STEP : (k + 1) * STEP] = part
        arrive(base + 1)
        left = ly[it, 0] + ly[it, 1] + ly[it, 2] + ly[it, 3]
        if it > 0:
            left = dot(six(inverse * 0.125), six_rows(left), 1, 0)

        high, middle, low = split(left)
        l9 = jnp.concatenate([jnp.concatenate([high, middle, low], axis=0)] * 3, axis=1)
        for k in range(half // STEP):
            part = dot(l9, m3[:, k * STEP : (k + 1) * STEP], 1, 0)
            part = part[:RANK] + part[RANK : 2 * RANK] + part[2 * RANK :]
            for n in range(STEP // LANES):
                tile = (k * STEP // LANES + n) * 4
                s[it, tile : tile + 4] = part[:, n * LANES : (n + 1) * LANES].reshape(4, 8, LANES)
        spans, at = [], 0
        for n, size_of in enumerate(PARTS):
            spans.append((6 + 3 * n, pl.ds(at, size_of), at, size_of))
            at = at + size_of
        for phase, span, at, size_of in spans:
            send(
                [s.at[it, pl.ds(9 * p // 2 + at, size_of)] for p in places], rs.at[it, mine, span],
                plane_peers, base + phase, rs.at[it, pl.ds(0, PLANE - 1), span],
            )

        other = jnp.concatenate([high, middle, low, high, middle, high], axis=1)
        square = dot(
            jnp.concatenate([high, high, high, middle, middle, low], axis=1),
            jnp.concatenate([other] * 4, axis=0), 1, 1,
        )
        lane = lax.broadcasted_iota(jnp.int32, (8, LANES), 1) // RANK
        packed = square[0:8]
        for r in range(1, 4):
            packed = jnp.where(lane == r, square[8 * r : 8 * r + 8], packed)
        gx[it, x] = packed
        send(gx.at[it, x], gx.at[it, x], x_peers, base + 2, gx.at[it, pl.ds(0, X - 1)])

        rs[it, mine] = s[it, pl.ds(9 * mine // 2, WINDOW)]
        for phase, span, at, size_of in spans:
            arrive(base + phase)
            piece = rs[it, 0, span]
            for p in range(1, PLANE):
                piece = piece + rs[it, p, span]
            zb[it, z, span] = piece
            send(zb.at[it, z, span], zb.at[it, z, span], z_peers, base + phase + 1, zb.at[it, pl.ds(0, Z - 1), span])
        arrive(base + 2)
        gz[it, z] = gx[it, 0] + gx[it, 1] + gx[it, 2] + gx[it, 3]
        send(gz.at[it, z], gz.at[it, z], z_peers, base + 3, gz.at[it, pl.ds(0, Z - 1)])
        for phase, span, at, size_of in spans:
            arrive(base + phase + 1)
            piece = zb[it, 0, span]
            for p in range(1, Z):
                piece = piece + zb[it, p, span]
            ag[it, mine, span] = piece
            send(ag.at[it, mine, span], ag.at[it, mine, span], plane_peers, base + phase + 2, ag.at[it, pl.ds(0, PLANE - 1), span])
        arrive(base + 3)
        gram = gz[it, 0]
        for p in range(1, Z):
            gram = gram + gz[it, p]
        inverse = lower_inverse(gram)
        for phase, span, at, size_of in spans:
            arrive(base + phase + 2)
    send(ag.at[ITERS - 1], back, [sibling], PHASES * ITERS - PHASES + 4, back)

    last = ITERS - 1
    inverse6 = six(inverse)
    high, middle, _ = split(dot(inverse6, six_rows(left), 1, 0))
    basis3 = jnp.concatenate([high, high, middle], axis=0).astype(F32).T.astype(BF16)
    inverse6 = (inverse6.astype(F32) * 0.125).astype(BF16)
    inverse_ref[...] = inverse6
    basis_ref[...] = basis3
    for k in range(half // STEP):
        finish(ag.at[last], k, columns_of(c, k, half), inverse6, basis3, g, e, rf, o)
    arrive(PHASES * ITERS - PHASES + 4)
    for whole, phase in sent:
        pltpu.make_async_copy(whole, whole, send_sem.at[phase]).wait()


def body(grads, errors, start_q):
    g, e = grads[0], errors[0]
    rows, columns = g.shape
    tiles = columns // 2 // LANES * 4
    steps = columns // STEP
    hbm, vmem = pl.BlockSpec(memory_space=pltpu.HBM), pl.BlockSpec(memory_space=pltpu.VMEM)
    held = pl.pallas_call(
        kernel,
        out_shape=(
            pltpu.VMEM((RANK, columns), F32),
            pltpu.VMEM((rows, columns), BF16),
            pltpu.VMEM((rows, columns), BF16),
            pltpu.VMEM((rows, columns), BF16),
            pltpu.VMEM((PLANE, WINDOW, 8, LANES), F32),
            pltpu.VMEM((RANK, 6 * RANK), BF16),
            pltpu.VMEM((rows, 3 * RANK), BF16),
        ),
        in_specs=[hbm] * 3,
        out_specs=(vmem,) * 7,
        scratch_shapes=[
            pltpu.VMEM((RANK, columns), F32),
            pltpu.VMEM((ITERS, RANK, rows), F32),
            pltpu.VMEM((ITERS, RANK, rows), F32),
            pltpu.VMEM((ITERS, Y, RANK, rows), F32),
            pltpu.VMEM((ITERS, X, 8, LANES), F32),
            pltpu.VMEM((ITERS, Z, 8, LANES), F32),
            pltpu.VMEM((ITERS, tiles, 8, LANES), F32),
            pltpu.VMEM((ITERS, PLANE, WINDOW, 8, LANES), F32),
            pltpu.VMEM((ITERS, Z, WINDOW, 8, LANES), F32),
            pltpu.VMEM((ITERS, PLANE, WINDOW, 8, LANES), F32),
            pltpu.VMEM((steps // 2, rows, STEP), F32),
            pltpu.VMEM((steps // 2, rows, STEP), F32),
            pltpu.VMEM((3 * rows, columns // 2), BF16),
            pltpu.SemaphoreType.DMA((3, steps)),
            pltpu.SemaphoreType.DMA((PHASES * ITERS + steps // 2,)),
            pltpu.SemaphoreType.DMA((PHASES * ITERS + steps // 2,)),
        ],
        name="power_iterations",
        compiler_params=pltpu.CompilerParams(collective_id=0, has_side_effects=True, vmem_limit_bytes=50 << 20),
        cost_estimate=pl.CostEstimate(flops=5 * 2 * rows * columns * RANK, bytes_accessed=6 * rows * columns, transcendentals=0),
    )(g, e, start_q.T)
    right, fresh = pl.pallas_call(
        last_kernel,
        out_shape=(jax.ShapeDtypeStruct((RANK, columns), F32), jax.ShapeDtypeStruct((rows, columns), BF16)),
        in_specs=[vmem] * 7,
        out_specs=(hbm, hbm),
        scratch_shapes=[
            pltpu.VMEM((RANK, columns), F32),
            pltpu.VMEM((rows, columns), BF16),
            pltpu.SemaphoreType.DMA((2 * steps,)),
        ],
        name="other_half",
        compiler_params=pltpu.CompilerParams(vmem_limit_bytes=16 << 20),
        cost_estimate=pl.CostEstimate(flops=2 * rows * columns * RANK, bytes_accessed=3 * rows * columns, transcendentals=0),
    )(*held)
    return right.T, fresh[None]


def solution(mesh):
    return jax.shard_map(
        body,
        mesh=mesh,
        in_specs=(P("dp", "vocab", None), P("dp", "vocab", None), P()),
        out_specs=(P(), P("dp", "vocab", None)),
        check_vma=False,
    )
```

```python
import functools

import jax
import jax.numpy as jnp
from jax import lax
from jax.experimental import pallas as pl
from jax.experimental.pallas import tpu as pltpu
from jax.sharding import PartitionSpec as P

MESH = pl.DeviceIdType.MESH
F32, BF16 = jnp.float32, jnp.bfloat16
ITERS = 2
RANK = 32
LANES = 128
STEP = 768
WINDOW = 2
Y, X, Z = 4, 4, 8
PLANE = Y * X
PHASES = 15
BULK = PHASES * ITERS


def split(value):
    high = value.astype(BF16)
    rest = value - high.astype(F32)
    middle = rest.astype(BF16)
    return high, middle, (rest - middle.astype(F32)).astype(BF16)


def dot(a, b, over_a, over_b):
    return lax.dot_general(a, b, (((over_a,), (over_b,)), ((), ())), preferred_element_type=F32)


def lower_inverse(packed):
    row = lax.broadcasted_iota(jnp.int32, (RANK, LANES), 0)
    lane = lax.broadcasted_iota(jnp.int32, (RANK, LANES), 1)
    turned = [packed if r == 1 else pltpu.roll(packed, (RANK - RANK * r) % LANES, 1) for r in range(4)]
    work = jnp.where(lane < RANK, jnp.where(lane == row, 1.0, 0.0), jnp.concatenate(turned, axis=0))
    rows = row[:, :1]
    pivots = jnp.ones((RANK, 1), F32)
    for j in range(RANK):
        column, pivot = work[:, RANK + j : RANK + j + 1], work[j : j + 1, RANK + j : RANK + j + 1]
        factor = jnp.where(rows > j, column / pivot, 0.0)
        pivots = jnp.where(rows == j, pivot, pivots)
        work = work - factor * work[j : j + 1, :]
    return (work * lax.rsqrt(pivots))[:, :RANK]


def six(value):
    high, middle, low = split(value)
    return jnp.concatenate([high, high, high, middle, middle, low], axis=1)


def six_rows(value):
    high, middle, low = split(value)
    return jnp.concatenate([high, middle, low, high, middle, high], axis=0)


def gathered(windows, k):
    parts = []
    for column in range(STEP // LANES):
        rows = []
        for r in range(4):
            pair, at = (column * 4 + r) // 3, (column * 4 + r) % 3
            rows.append(windows[k, 2 * pair + at // WINDOW, at if at < WINDOW else WINDOW - 1])
        parts.append(jnp.concatenate(rows, axis=0))
    return jnp.concatenate(parts, axis=1)


def finish(windows, k, where, inverse6, basis3, g, e, rf, o):
    right = dot(inverse6, six_rows(gathered(windows, k)), 1, 0)
    rf[:, where] = right
    high, middle, _ = split(right)
    approx = dot(basis3, jnp.concatenate([high, middle, high], axis=0), 1, 0)
    o[:, where] = (g[:, where].astype(F32) + e[:, where].astype(F32) - approx).astype(BF16)


def columns_of(which, k, half):
    return pl.ds(pl.multiple_of(which * half + k * STEP, LANES), STEP)


def last_kernel(rf_in, o_in, g, e, windows, inverse6, basis3, rf_hbm, o_hbm, rf, o, sems):
    c = lax.rem(lax.axis_index("dp"), 2)
    half = g.shape[1] // 2
    copies = []

    def write(src, dst, where):
        copies.append(pltpu.make_async_copy(src.at[:, where], dst.at[:, where], sems.at[len(copies)]))
        copies[-1].start()

    for k in range(half // STEP):
        write(o_in, o_hbm, columns_of(c, k, half))
        write(rf_in, rf_hbm, columns_of(c, k, half))
    for k in range(half // STEP):
        where = columns_of(1 - c, k, half)
        finish(windows, k, where, inverse6[...], basis3[...], g, e, rf, o)
        write(o, o_hbm, where)
        write(rf, rf_hbm, where)
    for copy in copies:
        copy.wait()


def kernel(
    g_hbm, e_hbm, q_hbm, rf, o, g, e, back, inverse_ref, basis_ref,
    q, lp, lr, ly, gx, gz, s, rs, zb, ag, mixed, mixed_in, m3,
    load_sem, send_sem, recv_sem,
):
    dp, vocab = lax.axis_index("dp"), lax.axis_index("vocab")
    y, c, x, z = dp // 2, lax.rem(dp, 2), vocab // Z, lax.rem(vocab, Z)
    mine = y * X + x
    columns = g.shape[1]
    half = columns // 2
    tiles = half // LANES

    def device(y, c, x, z):
        return (y * 2 + c, x * Z + z)

    sibling = device(y, 1 - c, x, z)
    y_peers = [device(lax.rem(y + k, Y), c, x, z) for k in (2, 1, 3)]
    x_peers = [device(y, c, lax.rem(x + k, X), z) for k in (2, 1, 3)]
    far = lambda k, size: min(k, size - k)
    z_peers = [device(y, c, x, lax.rem(z + k, Z)) for k in sorted(range(1, Z), key=lambda k: -far(k, Z))]
    steps = [(j, k) for j in range(Y) for k in range(X) if j + k > 0]
    steps.sort(key=lambda jk: -far(jk[0], Y) - far(jk[1], X))
    across = [(lax.rem(y + j, Y), lax.rem(x + k, X)) for j, k in steps]
    places = [j * X + k for j, k in across]
    plane_peers = [device(j, c, k, z) for j, k in across]

    chunks = [(which, k, columns_of(which, k, half)) for which in (1 - c, c) for k in range(half // STEP)]
    loads = []
    for n, (which, k, part) in enumerate(chunks):
        loads.append([
            pltpu.make_async_copy(hbm.at[:, part], vmem.at[:, part], load_sem.at[m, n])
            for m, (hbm, vmem) in enumerate(((q_hbm, q), (g_hbm, g), (e_hbm, e)))
        ])
        for copy in loads[-1]:
            copy.start()

    barrier = pltpu.get_barrier_semaphore()
    everyone = [sibling] + plane_peers + z_peers
    for peer in everyone:
        pl.semaphore_signal(barrier, inc=1, device_id=peer, device_id_type=MESH)

    sent = []

    pending = {}

    def send(src, dst, peers, phase, whole):
        pending[phase] = whole
        sources = src if isinstance(src, list) else [src] * len(peers)
        for source, peer in zip(sources, peers):
            pltpu.make_async_remote_copy(
                src_ref=source, dst_ref=dst, send_sem=send_sem.at[phase], recv_sem=recv_sem.at[phase],
                device_id=peer, device_id_type=MESH,
            ).start()

    def arrive(phase):
        whole = pending.pop(phase)
        pltpu.make_async_copy(whole, whole, recv_sem.at[phase]).wait()
        sent.append((whole, phase))

    def split3(q):
        return jnp.concatenate(split(q), axis=0)

    size = g.shape[0]
    inverse = None
    for it in range(ITERS):
        base = PHASES * it
        total = jnp.zeros((size, 3 * RANK), F32)
        if it == 0:
            for copies, (which, k, where) in zip(loads, chunks):
                for copy in copies:
                    copy.wait()
                q3 = split3(q[:, where])
                total = total + (dot(g[:, where], q3, 1, 1) + dot(e[:, where], q3, 1, 1))
            pl.semaphore_wait(barrier, len(everyone))
        else:
            for k in range(half // STEP):
                arrive(base - PHASES + 8 + 3 * k)
                part = dot(m3[:, k * STEP : (k + 1) * STEP], split3(gathered(ag.at[it - 1], k)), 1, 1)
                total = total + (part[:size] + part[size : 2 * size] + part[2 * size :])
        turned = jnp.concatenate([total, jnp.zeros((size, LANES - 3 * RANK), F32)], axis=1).T
        lp[it] = turned[:RANK] + turned[RANK : 2 * RANK] + turned[2 * RANK : 3 * RANK]
        send(lp.at[it], lr.at[it], [sibling], base, lr.at[it])
        if it == 0:
            for k in range(half // STEP):
                where = columns_of(1 - c, k, half)
                mixed[k] = g[:, where].astype(F32) + e[:, where].astype(F32)
                send(mixed.at[k], mixed_in.at[k], [sibling], BULK + k, mixed_in.at[k])
        arrive(base)
        ly[it, y] = lp[it] + lr[it]
        send(ly.at[it, y], ly.at[it, y], y_peers, base + 1, ly.at[it, pl.ds(0, Y - 1)])
        if it == 0:
            for k in range(half // STEP):
                where = columns_of(c, k, half)
                here = g[:, where].astype(F32) + e[:, where].astype(F32)
                arrive(BULK + k)
                for n, part in enumerate(split(here + mixed_in[k])):
                    m3[n * size : (n + 1) * size, k * STEP : (k + 1) * STEP] = part
        arrive(base + 1)
        left = ly[it, 0] + ly[it, 1] + ly[it, 2] + ly[it, 3]
        if it > 0:
            left = dot(six(inverse * 0.125), six_rows(left), 1, 0)

        high, middle, low = split(left)
        l9 = jnp.concatenate([jnp.concatenate([high, middle, low], axis=0)] * 3, axis=1)
        for k in range(half // STEP):
            part = dot(l9, m3[:, k * STEP : (k + 1) * STEP], 1, 0)
            part = part[:RANK] + part[RANK : 2 * RANK] + part[2 * RANK :]
            for n in range(STEP // LANES):
                s[it, k, 4 * n : 4 * n + 4] = part[:, n * LANES : (n + 1) * LANES].reshape(4, 8, LANES)
            send(
                [s.at[it, k, pl.ds(3 * p // 2, WINDOW)] for p in places], rs.at[it, k, mine],
                plane_peers, base + 6 + 3 * k, rs.at[it, k, pl.ds(0, PLANE - 1)],
            )

        other = jnp.concatenate([high, middle, low, high, middle, high], axis=1)
        square = dot(
            jnp.concatenate([high, high, high, middle, middle, low], axis=1),
            jnp.concatenate([other] * 4, axis=0), 1, 1,
        )
        lane = lax.broadcasted_iota(jnp.int32, (8, LANES), 1) // RANK
        packed = square[0:8]
        for r in range(1, 4):
            packed = jnp.where(lane == r, square[8 * r : 8 * r + 8], packed)
        gx[it, x] = packed
        send(gx.at[it, x], gx.at[it, x], x_peers, base + 2, gx.at[it, pl.ds(0, X - 1)])

        for k in range(half // STEP):
            rs[it, k, mine] = s[it, k, pl.ds(3 * mine // 2, WINDOW)]
            arrive(base + 6 + 3 * k)
            piece = rs[it, k, 0]
            for p in range(1, PLANE):
                piece = piece + rs[it, k, p]
            zb[it, k, z] = piece
            send(zb.at[it, k, z], zb.at[it, k, z], z_peers, base + 7 + 3 * k, zb.at[it, k, pl.ds(0, Z - 1)])
        arrive(base + 2)
        gz[it, z] = gx[it, 0] + gx[it, 1] + gx[it, 2] + gx[it, 3]
        send(gz.at[it, z], gz.at[it, z], z_peers, base + 3, gz.at[it, pl.ds(0, Z - 1)])
        for k in range(half // STEP):
            arrive(base + 7 + 3 * k)
            piece = zb[it, k, 0]
            for p in range(1, Z):
                piece = piece + zb[it, k, p]
            ag[it, k, mine] = piece
            send(ag.at[it, k, mine], ag.at[it, k, mine], plane_peers, base + 8 + 3 * k, ag.at[it, k, pl.ds(0, PLANE - 1)])
        arrive(base + 3)
        gram = gz[it, 0]
        for p in range(1, Z):
            gram = gram + gz[it, p]
        inverse = lower_inverse(gram)

    last = ITERS - 1
    inverse6 = six(inverse)
    high, middle, _ = split(dot(inverse6, six_rows(left), 1, 0))
    basis3 = jnp.concatenate([high, high, middle], axis=0).astype(F32).T.astype(BF16)
    inverse6 = (inverse6.astype(F32) * 0.125).astype(BF16)
    inverse_ref[...] = inverse6
    basis_ref[...] = basis3
    for k in range(half // STEP):
        arrive(PHASES * last + 8 + 3 * k)
        send(ag.at[last, k], back.at[k], [sibling], PHASES * last + 4, back)
        finish(ag.at[last], k, columns_of(c, k, half), inverse6, basis3, g, e, rf, o)
    arrive(PHASES * last + 4)
    for whole, phase in sent:
        pltpu.make_async_copy(whole, whole, send_sem.at[phase]).wait()


def body(grads, errors, start_q):
    g, e = grads[0], errors[0]
    rows, columns = g.shape
    steps = columns // STEP
    hbm, vmem = pl.BlockSpec(memory_space=pltpu.HBM), pl.BlockSpec(memory_space=pltpu.VMEM)
    held = pl.pallas_call(
        kernel,
        out_shape=(
            pltpu.VMEM((RANK, columns), F32),
            pltpu.VMEM((rows, columns), BF16),
            pltpu.VMEM((rows, columns), BF16),
            pltpu.VMEM((rows, columns), BF16),
            pltpu.VMEM((steps // 2, PLANE, WINDOW, 8, LANES), F32),
            pltpu.VMEM((RANK, 6 * RANK), BF16),
            pltpu.VMEM((rows, 3 * RANK), BF16),
        ),
        in_specs=[hbm] * 3,
        out_specs=(vmem,) * 7,
        scratch_shapes=[
            pltpu.VMEM((RANK, columns), F32),
            pltpu.VMEM((ITERS, RANK, rows), F32),
            pltpu.VMEM((ITERS, RANK, rows), F32),
            pltpu.VMEM((ITERS, Y, RANK, rows), F32),
            pltpu.VMEM((ITERS, X, 8, LANES), F32),
            pltpu.VMEM((ITERS, Z, 8, LANES), F32),
            pltpu.VMEM((ITERS, steps // 2, STEP // LANES * 4, 8, LANES), F32),
            pltpu.VMEM((ITERS, steps // 2, PLANE, WINDOW, 8, LANES), F32),
            pltpu.VMEM((ITERS, steps // 2, Z, WINDOW, 8, LANES), F32),
            pltpu.VMEM((ITERS, steps // 2, PLANE, WINDOW, 8, LANES), F32),
            pltpu.VMEM((steps // 2, rows, STEP), F32),
            pltpu.VMEM((steps // 2, rows, STEP), F32),
            pltpu.VMEM((3 * rows, columns // 2), BF16),
            pltpu.SemaphoreType.DMA((3, steps)),
            pltpu.SemaphoreType.DMA((PHASES * ITERS + steps // 2,)),
            pltpu.SemaphoreType.DMA((PHASES * ITERS + steps // 2,)),
        ],
        name="power_iterations",
        compiler_params=pltpu.CompilerParams(collective_id=0, has_side_effects=True, vmem_limit_bytes=50 << 20),
        cost_estimate=pl.CostEstimate(flops=5 * 2 * rows * columns * RANK, bytes_accessed=6 * rows * columns, transcendentals=0),
    )(g, e, start_q.T)
    right, fresh = pl.pallas_call(
        last_kernel,
        out_shape=(jax.ShapeDtypeStruct((RANK, columns), F32), jax.ShapeDtypeStruct((rows, columns), BF16)),
        in_specs=[vmem] * 7,
        out_specs=(hbm, hbm),
        scratch_shapes=[
            pltpu.VMEM((RANK, columns), F32),
            pltpu.VMEM((rows, columns), BF16),
            pltpu.SemaphoreType.DMA((2 * steps,)),
        ],
        name="other_half",
        compiler_params=pltpu.CompilerParams(vmem_limit_bytes=16 << 20),
        cost_estimate=pl.CostEstimate(flops=2 * rows * columns * RANK, bytes_accessed=3 * rows * columns, transcendentals=0),
    )(*held)
    return right.T, fresh[None]


def solution(mesh):
    return jax.shard_map(
        body,
        mesh=mesh,
        in_specs=(P("dp", "vocab", None), P("dp", "vocab", None), P()),
        out_specs=(P(), P("dp", "vocab", None)),
        check_vma=False,
    )
```

```python
import functools

import jax
import jax.numpy as jnp
from jax import lax
from jax.experimental import pallas as pl
from jax.experimental.pallas import tpu as pltpu
from jax.sharding import PartitionSpec as P

MESH = pl.DeviceIdType.MESH
F32, BF16 = jnp.float32, jnp.bfloat16
ITERS = 2
RANK = 32
LANES = 128
STEP = 768
PARTS = ((0, 1024, 2), (1024, 768, 2), (1792, 512, 1))
TILES = tuple(width // 32 for _, width, _ in PARTS)
Y, X, Z = 4, 4, 8
PLANE = Y * X
PHASES = 16
BULK = PHASES * ITERS


def split(value):
    high = value.astype(BF16)
    rest = value - high.astype(F32)
    middle = rest.astype(BF16)
    return high, middle, (rest - middle.astype(F32)).astype(BF16)


def dot(a, b, over_a, over_b):
    return lax.dot_general(a, b, (((over_a,), (over_b,)), ((), ())), preferred_element_type=F32)


def lower_inverse(packed):
    row = lax.broadcasted_iota(jnp.int32, (RANK, LANES), 0)
    lane = lax.broadcasted_iota(jnp.int32, (RANK, LANES), 1)
    turned = [packed if r == 1 else pltpu.roll(packed, (RANK - RANK * r) % LANES, 1) for r in range(4)]
    work = jnp.where(lane < RANK, jnp.where(lane == row, 1.0, 0.0), jnp.concatenate(turned, axis=0))
    rows = row[:, :1]
    pivots = jnp.ones((RANK, 1), F32)
    for j in range(RANK):
        column, pivot = work[:, RANK + j : RANK + j + 1], work[j : j + 1, RANK + j : RANK + j + 1]
        factor = jnp.where(rows > j, column / pivot, 0.0)
        pivots = jnp.where(rows == j, pivot, pivots)
        work = work - factor * work[j : j + 1, :]
    return (work * lax.rsqrt(pivots))[:, :RANK]


def six(value):
    high, middle, low = split(value)
    return jnp.concatenate([high, high, high, middle, middle, low], axis=1)


def six_rows(value):
    high, middle, low = split(value)
    return jnp.concatenate([high, middle, low, high, middle, high], axis=0)


def gathered(windows, k):
    parts = []
    for column in range(TILES[k] // 4):
        rows = []
        for tile in range(4 * column, 4 * column + 4):
            place = next(p for p in range(PLANE) if tile - p * TILES[k] // PLANE < PARTS[k][2])
            rows.append(windows[k, place, tile - place * TILES[k] // PLANE])
        parts.append(jnp.concatenate(rows, axis=0))
    return jnp.concatenate(parts, axis=1)


def finish(windows, k, where, inverse6, basis3, g, e, rf, o):
    right = dot(inverse6, six_rows(gathered(windows, k)), 1, 0)
    rf[:, where] = right
    high, middle, _ = split(right)
    approx = dot(basis3, jnp.concatenate([high, middle, high], axis=0), 1, 0)
    o[:, where] = (g[:, where].astype(F32) + e[:, where].astype(F32) - approx).astype(BF16)


def columns_of(which, k, half):
    return pl.ds(pl.multiple_of(which * half + k * STEP, LANES), STEP)


def part_of(which, k, half):
    return pl.ds(pl.multiple_of(which * half + PARTS[k][0], LANES), PARTS[k][1])


def last_kernel(rf_in, o_in, g, e, windows, inverse6, basis3, rf_hbm, o_hbm, rf, o, sems):
    c = lax.rem(lax.axis_index("dp"), 2)
    half = g.shape[1] // 2
    copies = []

    def write(src, dst, where):
        copies.append(pltpu.make_async_copy(src.at[:, where], dst.at[:, where], sems.at[len(copies)]))
        copies[-1].start()

    for k in range(len(PARTS)):
        write(o_in, o_hbm, part_of(c, k, half))
        write(rf_in, rf_hbm, part_of(c, k, half))
    for k in range(len(PARTS)):
        where = part_of(1 - c, k, half)
        finish(windows, k, where, inverse6[...], basis3[...], g, e, rf, o)
        write(o, o_hbm, where)
        write(rf, rf_hbm, where)
    for copy in copies:
        copy.wait()


def kernel(
    g_hbm, e_hbm, q_hbm, rf, o, g, e, back, inverse_ref, basis_ref,
    q, lp, lr, ly, gx, gz, s, rs, zb, ag, mixed, mixed_in, m3,
    load_sem, send_sem, recv_sem,
):
    dp, vocab = lax.axis_index("dp"), lax.axis_index("vocab")
    y, c, x, z = dp // 2, lax.rem(dp, 2), vocab // Z, lax.rem(vocab, Z)
    mine = y * X + x
    columns = g.shape[1]
    half = columns // 2
    tiles = half // LANES

    def device(y, c, x, z):
        return (y * 2 + c, x * Z + z)

    sibling = device(y, 1 - c, x, z)
    y_peers = [device(lax.rem(y + k, Y), c, x, z) for k in (2, 1, 3)]
    x_peers = [device(y, c, lax.rem(x + k, X), z) for k in (2, 1, 3)]
    far = lambda k, size: min(k, size - k)
    z_peers = [device(y, c, x, lax.rem(z + k, Z)) for k in sorted(range(1, Z), key=lambda k: -far(k, Z))]
    steps = [(j, k) for j in range(Y) for k in range(X) if j + k > 0]
    steps.sort(key=lambda jk: -far(jk[0], Y) - far(jk[1], X))
    across = [(lax.rem(y + j, Y), lax.rem(x + k, X)) for j, k in steps]
    places = [j * X + k for j, k in across]
    plane_peers = [device(j, c, k, z) for j, k in across]

    chunks = [(which, k, columns_of(which, k, half)) for which in (1 - c, c) for k in range(half // STEP)]
    loads = []
    for n, (which, k, part) in enumerate(chunks):
        loads.append([
            pltpu.make_async_copy(hbm.at[:, part], vmem.at[:, part], load_sem.at[m, n])
            for m, (hbm, vmem) in enumerate(((q_hbm, q), (g_hbm, g), (e_hbm, e)))
        ])
        for copy in loads[-1]:
            copy.start()

    barrier = pltpu.get_barrier_semaphore()
    everyone = [sibling] + plane_peers + z_peers
    for peer in everyone:
        pl.semaphore_signal(barrier, inc=1, device_id=peer, device_id_type=MESH)

    sent = []

    pending = {}

    def send(src, dst, peers, phase, whole):
        pending[phase] = whole
        sources = src if isinstance(src, list) else [src] * len(peers)
        for source, peer in zip(sources, peers):
            pltpu.make_async_remote_copy(
                src_ref=source, dst_ref=dst, send_sem=send_sem.at[phase], recv_sem=recv_sem.at[phase],
                device_id=peer, device_id_type=MESH,
            ).start()

    def arrive(phase):
        whole = pending.pop(phase)
        pltpu.make_async_copy(whole, whole, recv_sem.at[phase]).wait()
        sent.append((whole, phase))

    def split3(q):
        return jnp.concatenate(split(q), axis=0)

    size = g.shape[0]
    inverse = None
    for it in range(ITERS):
        base = PHASES * it
        total = jnp.zeros((size, 3 * RANK), F32)
        if it == 0:
            for copies, (which, k, where) in zip(loads, chunks):
                for copy in copies:
                    copy.wait()
                q3 = split3(q[:, where])
                total = total + (dot(g[:, where], q3, 1, 1) + dot(e[:, where], q3, 1, 1))
            pl.semaphore_wait(barrier, len(everyone))
        else:
            for k, (first, width, _) in enumerate(PARTS):
                arrive(base - PHASES + 8 + 3 * k)
                part = dot(m3[:, first : first + width], split3(gathered(ag.at[it - 1], k)), 1, 1)
                total = total + (part[:size] + part[size : 2 * size] + part[2 * size :])
        turned = jnp.concatenate([total, jnp.zeros((size, LANES - 3 * RANK), F32)], axis=1).T
        lp[it] = turned[:RANK] + turned[RANK : 2 * RANK] + turned[2 * RANK : 3 * RANK]
        send(lp.at[it], lr.at[it], [sibling], base, lr.at[it])
        if it == 0:
            for k in range(half // STEP):
                where = columns_of(1 - c, k, half)
                mixed[k] = g[:, where].astype(F32) + e[:, where].astype(F32)
                send(mixed.at[k], mixed_in.at[k], [sibling], BULK + k, mixed_in.at[k])
        arrive(base)
        ly[it, y] = lp[it] + lr[it]
        send(ly.at[it, y], ly.at[it, y], y_peers, base + 1, ly.at[it, pl.ds(0, Y - 1)])
        if it == 0:
            for k in range(half // STEP):
                where = columns_of(c, k, half)
                here = g[:, where].astype(F32) + e[:, where].astype(F32)
                arrive(BULK + k)
                for n, part in enumerate(split(here + mixed_in[k])):
                    m3[n * size : (n + 1) * size, k * STEP : (k + 1) * STEP] = part
        arrive(base + 1)
        left = ly[it, 0] + ly[it, 1] + ly[it, 2] + ly[it, 3]
        if it > 0:
            left = dot(six(inverse * 0.125), six_rows(left), 1, 0)

        high, middle, low = split(left)
        l9 = jnp.concatenate([jnp.concatenate([high, middle, low], axis=0)] * 3, axis=1)
        for k, (first, width, window) in enumerate(PARTS):
            part = dot(l9, m3[:, first : first + width], 1, 0)
            part = part[:RANK] + part[RANK : 2 * RANK] + part[2 * RANK :]
            for n in range(width // LANES):
                s[it, k, 4 * n : 4 * n + 4] = part[:, n * LANES : (n + 1) * LANES].reshape(4, 8, LANES)
            send(
                [s.at[it, k, pl.ds(p * TILES[k] // PLANE, window)] for p in places], rs.at[it, k, mine, pl.ds(0, window)],
                plane_peers, base + 6 + 3 * k, rs.at[it, k, pl.ds(0, PLANE - 1), pl.ds(0, window)],
            )

        other = jnp.concatenate([high, middle, low, high, middle, high], axis=1)
        square = dot(
            jnp.concatenate([high, high, high, middle, middle, low], axis=1),
            jnp.concatenate([other] * 4, axis=0), 1, 1,
        )
        lane = lax.broadcasted_iota(jnp.int32, (8, LANES), 1) // RANK
        packed = square[0:8]
        for r in range(1, 4):
            packed = jnp.where(lane == r, square[8 * r : 8 * r + 8], packed)
        gx[it, x] = packed
        send(gx.at[it, x], gx.at[it, x], x_peers, base + 2, gx.at[it, pl.ds(0, X - 1)])

        for k, (_, _, window) in enumerate(PARTS):
            span = pl.ds(0, window)
            rs[it, k, mine, span] = s[it, k, pl.ds(mine * TILES[k] // PLANE, window)]
            arrive(base + 6 + 3 * k)
            piece = rs[it, k, 0, span]
            for p in range(1, PLANE):
                piece = piece + rs[it, k, p, span]
            zb[it, k, z, span] = piece
            send(
                zb.at[it, k, z, span], zb.at[it, k, z, span],
                z_peers, base + 7 + 3 * k, zb.at[it, k, pl.ds(0, Z - 1), span],
            )
        arrive(base + 2)
        gz[it, z] = gx[it, 0] + gx[it, 1] + gx[it, 2] + gx[it, 3]
        send(gz.at[it, z], gz.at[it, z], z_peers, base + 3, gz.at[it, pl.ds(0, Z - 1)])
        for k, (_, _, window) in enumerate(PARTS):
            span = pl.ds(0, window)
            arrive(base + 7 + 3 * k)
            piece = zb[it, k, 0, span]
            for p in range(1, Z):
                piece = piece + zb[it, k, p, span]
            ag[it, k, mine, span] = piece
            send(
                ag.at[it, k, mine, span], ag.at[it, k, mine, span],
                plane_peers, base + 8 + 3 * k, ag.at[it, k, pl.ds(0, PLANE - 1), span],
            )
        arrive(base + 3)
        gram = gz[it, 0]
        for p in range(1, Z):
            gram = gram + gz[it, p]
        inverse = lower_inverse(gram)

    last = ITERS - 1
    inverse6 = six(inverse)
    high, middle, _ = split(dot(inverse6, six_rows(left), 1, 0))
    basis3 = jnp.concatenate([high, high, middle], axis=0).astype(F32).T.astype(BF16)
    inverse6 = (inverse6.astype(F32) * 0.125).astype(BF16)
    inverse_ref[...] = inverse6
    basis_ref[...] = basis3
    for k, (_, _, window) in enumerate(PARTS):
        span = pl.ds(0, window)
        arrive(PHASES * last + 8 + 3 * k)
        send(ag.at[last, k, :, span], back.at[k, :, span], [sibling], (4, 5, 15)[k] + PHASES * last, back.at[k, :, span])
        finish(ag.at[last], k, part_of(c, k, half), inverse6, basis3, g, e, rf, o)
    for phase in (4, 5, 15):
        arrive(PHASES * last + phase)
    for whole, phase in sent:
        pltpu.make_async_copy(whole, whole, send_sem.at[phase]).wait()


def body(grads, errors, start_q):
    g, e = grads[0], errors[0]
    rows, columns = g.shape
    steps = columns // STEP
    hbm, vmem = pl.BlockSpec(memory_space=pltpu.HBM), pl.BlockSpec(memory_space=pltpu.VMEM)
    held = pl.pallas_call(
        kernel,
        out_shape=(
            pltpu.VMEM((RANK, columns), F32),
            pltpu.VMEM((rows, columns), BF16),
            pltpu.VMEM((rows, columns), BF16),
            pltpu.VMEM((rows, columns), BF16),
            pltpu.VMEM((len(PARTS), PLANE, 2, 8, LANES), F32),
            pltpu.VMEM((RANK, 6 * RANK), BF16),
            pltpu.VMEM((rows, 3 * RANK), BF16),
        ),
        in_specs=[hbm] * 3,
        out_specs=(vmem,) * 7,
        scratch_shapes=[
            pltpu.VMEM((RANK, columns), F32),
            pltpu.VMEM((ITERS, RANK, rows), F32),
            pltpu.VMEM((ITERS, RANK, rows), F32),
            pltpu.VMEM((ITERS, Y, RANK, rows), F32),
            pltpu.VMEM((ITERS, X, 8, LANES), F32),
            pltpu.VMEM((ITERS, Z, 8, LANES), F32),
            pltpu.VMEM((ITERS, len(PARTS), max(TILES), 8, LANES), F32),
            pltpu.VMEM((ITERS, len(PARTS), PLANE, 2, 8, LANES), F32),
            pltpu.VMEM((ITERS, len(PARTS), Z, 2, 8, LANES), F32),
            pltpu.VMEM((ITERS, len(PARTS), PLANE, 2, 8, LANES), F32),
            pltpu.VMEM((steps // 2, rows, STEP), F32),
            pltpu.VMEM((steps // 2, rows, STEP), F32),
            pltpu.VMEM((3 * rows, columns // 2), BF16),
            pltpu.SemaphoreType.DMA((3, steps)),
            pltpu.SemaphoreType.DMA((PHASES * ITERS + steps // 2,)),
            pltpu.SemaphoreType.DMA((PHASES * ITERS + steps // 2,)),
        ],
        name="power_iterations",
        compiler_params=pltpu.CompilerParams(collective_id=0, has_side_effects=True, vmem_limit_bytes=50 << 20),
        cost_estimate=pl.CostEstimate(flops=5 * 2 * rows * columns * RANK, bytes_accessed=6 * rows * columns, transcendentals=0),
    )(g, e, start_q.T)
    right, fresh = pl.pallas_call(
        last_kernel,
        out_shape=(jax.ShapeDtypeStruct((RANK, columns), F32), jax.ShapeDtypeStruct((rows, columns), BF16)),
        in_specs=[vmem] * 7,
        out_specs=(hbm, hbm),
        scratch_shapes=[
            pltpu.VMEM((RANK, columns), F32),
            pltpu.VMEM((rows, columns), BF16),
            pltpu.SemaphoreType.DMA((2 * steps,)),
        ],
        name="other_half",
        compiler_params=pltpu.CompilerParams(vmem_limit_bytes=16 << 20),
        cost_estimate=pl.CostEstimate(flops=2 * rows * columns * RANK, bytes_accessed=3 * rows * columns, transcendentals=0),
    )(*held)
    return right.T, fresh[None]


def solution(mesh):
    return jax.shard_map(
        body,
        mesh=mesh,
        in_specs=(P("dp", "vocab", None), P("dp", "vocab", None), P()),
        out_specs=(P(), P("dp", "vocab", None)),
        check_vma=False,
    )
```

```python
import functools

import jax
import jax.numpy as jnp
from jax import lax
from jax.experimental import pallas as pl
from jax.experimental.pallas import tpu as pltpu
from jax.sharding import PartitionSpec as P

MESH = pl.DeviceIdType.MESH
F32, BF16 = jnp.float32, jnp.bfloat16
ITERS = 2
RANK = 32
LANES = 128
STEP = 768
PARTS = ((0, 1024, 2), (1024, 768, 2), (1792, 512, 1))
TILES = tuple(width // 32 for _, width, _ in PARTS)
Y, X, Z = 4, 4, 8
PLANE = Y * X
PHASES = 16
BULK = PHASES * ITERS


def split(value):
    high = value.astype(BF16)
    rest = value - high.astype(F32)
    middle = rest.astype(BF16)
    return high, middle, (rest - middle.astype(F32)).astype(BF16)


def dot(a, b, over_a, over_b):
    return lax.dot_general(a, b, (((over_a,), (over_b,)), ((), ())), preferred_element_type=F32)


def lower_inverse(packed):
    row = lax.broadcasted_iota(jnp.int32, (RANK, LANES), 0)
    lane = lax.broadcasted_iota(jnp.int32, (RANK, LANES), 1)
    turned = [packed if r == 1 else pltpu.roll(packed, (RANK - RANK * r) % LANES, 1) for r in range(4)]
    work = jnp.where(lane < RANK, jnp.where(lane == row, 1.0, 0.0), jnp.concatenate(turned, axis=0))
    rows = row[:, :1]
    pivots = jnp.ones((RANK, 1), F32)
    for j in range(RANK):
        column, pivot = work[:, RANK + j : RANK + j + 1], work[j : j + 1, RANK + j : RANK + j + 1]
        factor = jnp.where(rows > j, column / pivot, 0.0)
        pivots = jnp.where(rows == j, pivot, pivots)
        work = work - factor * work[j : j + 1, :]
    return (work * lax.rsqrt(pivots))[:, :RANK]


def six(value):
    high, middle, low = split(value)
    return jnp.concatenate([high, high, high, middle, middle, low], axis=1)


def six_rows(value):
    high, middle, low = split(value)
    return jnp.concatenate([high, middle, low, high, middle, high], axis=0)


def gathered(windows, k):
    parts = []
    for column in range(TILES[k] // 4):
        rows = []
        for tile in range(4 * column, 4 * column + 4):
            place = next(p for p in range(PLANE) if tile - p * TILES[k] // PLANE < PARTS[k][2])
            rows.append(windows[k, place, tile - place * TILES[k] // PLANE])
        parts.append(jnp.concatenate(rows, axis=0))
    return jnp.concatenate(parts, axis=1)


def finish(windows, k, where, inverse6, basis3, g, e, rf, o):
    right = dot(inverse6, six_rows(gathered(windows, k)), 1, 0)
    rf[:, where] = right
    high, middle, _ = split(right)
    approx = dot(basis3, jnp.concatenate([high, middle, high], axis=0), 1, 0)
    o[:, where] = (g[:, where].astype(F32) + e[:, where].astype(F32) - approx).astype(BF16)


def columns_of(which, k, half):
    return pl.ds(pl.multiple_of(which * half + k * STEP, LANES), STEP)


def part_of(which, k, half):
    return pl.ds(pl.multiple_of(which * half + PARTS[k][0], LANES), PARTS[k][1])


def last_kernel(rf_in, o_in, g, e, windows, inverse6, basis3, rf_hbm, o_hbm, rf, o, sems):
    c = lax.rem(lax.axis_index("dp"), 2)
    half = g.shape[1] // 2
    copies = []

    def write(src, dst, where):
        copies.append(pltpu.make_async_copy(src.at[:, where], dst.at[:, where], sems.at[len(copies)]))
        copies[-1].start()

    for k in range(len(PARTS)):
        write(o_in, o_hbm, part_of(c, k, half))
        write(rf_in, rf_hbm, part_of(c, k, half))
    for k in range(len(PARTS)):
        where = part_of(1 - c, k, half)
        finish(windows, k, where, inverse6[...], basis3[...], g, e, rf, o)
        write(o, o_hbm, where)
        write(rf, rf_hbm, where)
    for copy in copies:
        copy.wait()


def kernel(
    g_hbm, e_hbm, q_hbm, rf, o, g, e, back, inverse_ref, basis_ref,
    q, lp, lr, ly, gx, gz, s, rs, zb, ag, mixed, mixed_in, m3,
    load_sem, send_sem, recv_sem,
):
    dp, vocab = lax.axis_index("dp"), lax.axis_index("vocab")
    y, c, x, z = dp // 2, lax.rem(dp, 2), vocab // Z, lax.rem(vocab, Z)
    mine = y * X + x
    columns = g.shape[1]
    half = columns // 2
    tiles = half // LANES

    def device(y, c, x, z):
        return (y * 2 + c, x * Z + z)

    sibling = device(y, 1 - c, x, z)
    y_peers = [device(lax.rem(y + k, Y), c, x, z) for k in (2, 1, 3)]
    x_peers = [device(y, c, lax.rem(x + k, X), z) for k in (2, 1, 3)]
    far = lambda k, size: min(k, size - k)
    z_peers = [device(y, c, x, lax.rem(z + k, Z)) for k in sorted(range(1, Z), key=lambda k: -far(k, Z))]
    steps = [(j, k) for j in range(Y) for k in range(X) if j + k > 0]
    steps.sort(key=lambda jk: -far(jk[0], Y) - far(jk[1], X))
    across = [(lax.rem(y + j, Y), lax.rem(x + k, X)) for j, k in steps]
    places = [j * X + k for j, k in across]
    plane_peers = [device(j, c, k, z) for j, k in across]

    chunks = [(which, k, columns_of(which, k, half)) for which in (1 - c, c) for k in range(half // STEP)]
    loads = []
    for n, (which, k, part) in enumerate(chunks):
        loads.append([
            pltpu.make_async_copy(hbm.at[:, part], vmem.at[:, part], load_sem.at[m, n])
            for m, (hbm, vmem) in enumerate(((q_hbm, q), (g_hbm, g), (e_hbm, e)))
        ])
        for copy in loads[-1]:
            copy.start()

    barrier = pltpu.get_barrier_semaphore()
    everyone = [sibling] + plane_peers + z_peers
    for peer in everyone:
        pl.semaphore_signal(barrier, inc=1, device_id=peer, device_id_type=MESH)

    sent = []

    pending = {}

    def send(src, dst, peers, phase, whole):
        pending[phase] = whole
        sources = src if isinstance(src, list) else [src] * len(peers)
        for source, peer in zip(sources, peers):
            pltpu.make_async_remote_copy(
                src_ref=source, dst_ref=dst, send_sem=send_sem.at[phase], recv_sem=recv_sem.at[phase],
                device_id=peer, device_id_type=MESH,
            ).start()

    def arrive(phase):
        whole = pending.pop(phase)
        pltpu.make_async_copy(whole, whole, recv_sem.at[phase]).wait()
        sent.append((whole, phase))

    def drain():
        while sent:
            whole, phase = sent.pop()
            pltpu.make_async_copy(whole, whole, send_sem.at[phase]).wait()

    def split3(q):
        return jnp.concatenate(split(q), axis=0)

    size = g.shape[0]
    inverse = None
    for it in range(ITERS):
        base = PHASES * it
        total = jnp.zeros((size, 3 * RANK), F32)
        if it == 0:
            for copies, (which, k, where) in zip(loads, chunks):
                for copy in copies:
                    copy.wait()
                q3 = split3(q[:, where])
                total = total + (dot(g[:, where], q3, 1, 1) + dot(e[:, where], q3, 1, 1))
            pl.semaphore_wait(barrier, len(everyone))
        else:
            for k, (first, width, _) in enumerate(PARTS):
                arrive(base - PHASES + 8 + 3 * k)
                part = dot(m3[:, first : first + width], split3(gathered(ag.at[it - 1], k)), 1, 1)
                total = total + (part[:size] + part[size : 2 * size] + part[2 * size :])
        turned = jnp.concatenate([total, jnp.zeros((size, LANES - 3 * RANK), F32)], axis=1).T
        lp[it] = turned[:RANK] + turned[RANK : 2 * RANK] + turned[2 * RANK : 3 * RANK]
        send(lp.at[it], lr.at[it], [sibling], base, lr.at[it])
        if it == 0:
            for k in range(half // STEP):
                where = columns_of(1 - c, k, half)
                mixed[k] = g[:, where].astype(F32) + e[:, where].astype(F32)
                send(mixed.at[k], mixed_in.at[k], [sibling], BULK + k, mixed_in.at[k])
        arrive(base)
        ly[it, y] = lp[it] + lr[it]
        send(ly.at[it, y], ly.at[it, y], y_peers, base + 1, ly.at[it, pl.ds(0, Y - 1)])
        if it == 0:
            for k in range(half // STEP):
                where = columns_of(c, k, half)
                here = g[:, where].astype(F32) + e[:, where].astype(F32)
                arrive(BULK + k)
                for n, part in enumerate(split(here + mixed_in[k])):
                    m3[n * size : (n + 1) * size, k * STEP : (k + 1) * STEP] = part
        arrive(base + 1)
        left = ly[it, 0] + ly[it, 1] + ly[it, 2] + ly[it, 3]
        if it > 0:
            left = dot(six(inverse * 0.125), six_rows(left), 1, 0)

        high, middle, low = split(left)
        l9 = jnp.concatenate([jnp.concatenate([high, middle, low], axis=0)] * 3, axis=1)
        for k, (first, width, window) in enumerate(PARTS):
            part = dot(l9, m3[:, first : first + width], 1, 0)
            part = part[:RANK] + part[RANK : 2 * RANK] + part[2 * RANK :]
            for n in range(width // LANES):
                s[it, k, 4 * n : 4 * n + 4] = part[:, n * LANES : (n + 1) * LANES].reshape(4, 8, LANES)
            send(
                [s.at[it, k, pl.ds(p * TILES[k] // PLANE, window)] for p in places], rs.at[it, k, mine, pl.ds(0, window)],
                plane_peers, base + 6 + 3 * k, rs.at[it, k, pl.ds(0, PLANE - 1), pl.ds(0, window)],
            )

        other = jnp.concatenate([high, middle, low, high, middle, high], axis=1)
        square = dot(
            jnp.concatenate([high, high, high, middle, middle, low], axis=1),
            jnp.concatenate([other] * 4, axis=0), 1, 1,
        )
        lane = lax.broadcasted_iota(jnp.int32, (8, LANES), 1) // RANK
        packed = square[0:8]
        for r in range(1, 4):
            packed = jnp.where(lane == r, square[8 * r : 8 * r + 8], packed)
        gx[it, x] = packed
        send(gx.at[it, x], gx.at[it, x], x_peers, base + 2, gx.at[it, pl.ds(0, X - 1)])

        for k, (_, _, window) in enumerate(PARTS):
            span = pl.ds(0, window)
            rs[it, k, mine, span] = s[it, k, pl.ds(mine * TILES[k] // PLANE, window)]
            arrive(base + 6 + 3 * k)
            piece = rs[it, k, 0, span]
            for p in range(1, PLANE):
                piece = piece + rs[it, k, p, span]
            zb[it, k, z, span] = piece
            send(
                zb.at[it, k, z, span], zb.at[it, k, z, span],
                z_peers, base + 7 + 3 * k, zb.at[it, k, pl.ds(0, Z - 1), span],
            )
        arrive(base + 2)
        gz[it, z] = gx[it, 0] + gx[it, 1] + gx[it, 2] + gx[it, 3]
        send(gz.at[it, z], gz.at[it, z], z_peers, base + 3, gz.at[it, pl.ds(0, Z - 1)])
        drain()
        for k, (_, _, window) in enumerate(PARTS):
            span = pl.ds(0, window)
            arrive(base + 7 + 3 * k)
            piece = zb[it, k, 0, span]
            for p in range(1, Z):
                piece = piece + zb[it, k, p, span]
            ag[it, k, mine, span] = piece
            send(
                ag.at[it, k, mine, span], ag.at[it, k, mine, span],
                plane_peers, base + 8 + 3 * k, ag.at[it, k, pl.ds(0, PLANE - 1), span],
            )
        arrive(base + 3)
        gram = gz[it, 0]
        for p in range(1, Z):
            gram = gram + gz[it, p]
        inverse = lower_inverse(gram)

    last = ITERS - 1
    inverse6 = six(inverse)
    high, middle, _ = split(dot(inverse6, six_rows(left), 1, 0))
    basis3 = jnp.concatenate([high, high, middle], axis=0).astype(F32).T.astype(BF16)
    inverse6 = (inverse6.astype(F32) * 0.125).astype(BF16)
    inverse_ref[...] = inverse6
    basis_ref[...] = basis3
    for k, (_, _, window) in enumerate(PARTS):
        span = pl.ds(0, window)
        arrive(PHASES * last + 8 + 3 * k)
        send(ag.at[last, k, :, span], back.at[k, :, span], [sibling], (4, 5, 15)[k] + PHASES * last, back.at[k, :, span])
        finish(ag.at[last], k, part_of(c, k, half), inverse6, basis3, g, e, rf, o)
    for phase in (4, 5, 15):
        arrive(PHASES * last + phase)
    drain()


def body(grads, errors, start_q):
    g, e = grads[0], errors[0]
    rows, columns = g.shape
    steps = columns // STEP
    hbm, vmem = pl.BlockSpec(memory_space=pltpu.HBM), pl.BlockSpec(memory_space=pltpu.VMEM)
    held = pl.pallas_call(
        kernel,
        out_shape=(
            pltpu.VMEM((RANK, columns), F32),
            pltpu.VMEM((rows, columns), BF16),
            pltpu.VMEM((rows, columns), BF16),
            pltpu.VMEM((rows, columns), BF16),
            pltpu.VMEM((len(PARTS), PLANE, 2, 8, LANES), F32),
            pltpu.VMEM((RANK, 6 * RANK), BF16),
            pltpu.VMEM((rows, 3 * RANK), BF16),
        ),
        in_specs=[hbm] * 3,
        out_specs=(vmem,) * 7,
        scratch_shapes=[
            pltpu.VMEM((RANK, columns), F32),
            pltpu.VMEM((ITERS, RANK, rows), F32),
            pltpu.VMEM((ITERS, RANK, rows), F32),
            pltpu.VMEM((ITERS, Y, RANK, rows), F32),
            pltpu.VMEM((ITERS, X, 8, LANES), F32),
            pltpu.VMEM((ITERS, Z, 8, LANES), F32),
            pltpu.VMEM((ITERS, len(PARTS), max(TILES), 8, LANES), F32),
            pltpu.VMEM((ITERS, len(PARTS), PLANE, 2, 8, LANES), F32),
            pltpu.VMEM((ITERS, len(PARTS), Z, 2, 8, LANES), F32),
            pltpu.VMEM((ITERS, len(PARTS), PLANE, 2, 8, LANES), F32),
            pltpu.VMEM((steps // 2, rows, STEP), F32),
            pltpu.VMEM((steps // 2, rows, STEP), F32),
            pltpu.VMEM((3 * rows, columns // 2), BF16),
            pltpu.SemaphoreType.DMA((3, steps)),
            pltpu.SemaphoreType.DMA((PHASES * ITERS + steps // 2,)),
            pltpu.SemaphoreType.DMA((PHASES * ITERS + steps // 2,)),
        ],
        name="power_iterations",
        compiler_params=pltpu.CompilerParams(collective_id=0, has_side_effects=True, vmem_limit_bytes=50 << 20),
        cost_estimate=pl.CostEstimate(flops=5 * 2 * rows * columns * RANK, bytes_accessed=6 * rows * columns, transcendentals=0),
    )(g, e, start_q.T)
    right, fresh = pl.pallas_call(
        last_kernel,
        out_shape=(jax.ShapeDtypeStruct((RANK, columns), F32), jax.ShapeDtypeStruct((rows, columns), BF16)),
        in_specs=[vmem] * 7,
        out_specs=(hbm, hbm),
        scratch_shapes=[
            pltpu.VMEM((RANK, columns), F32),
            pltpu.VMEM((rows, columns), BF16),
            pltpu.SemaphoreType.DMA((2 * steps,)),
        ],
        name="other_half",
        compiler_params=pltpu.CompilerParams(vmem_limit_bytes=16 << 20),
        cost_estimate=pl.CostEstimate(flops=2 * rows * columns * RANK, bytes_accessed=3 * rows * columns, transcendentals=0),
    )(*held)
    return right.T, fresh[None]


def solution(mesh):
    return jax.shard_map(
        body,
        mesh=mesh,
        in_specs=(P("dp", "vocab", None), P("dp", "vocab", None), P()),
        out_specs=(P(), P("dp", "vocab", None)),
        check_vma=False,
    )
```
